256 devices in a mesh: grp: 16 (over x_lo, y, core), blk: 16 (over x_hi, z).
Axes of the slice: x: 4 (x_hi: 2, x_lo: 2; x = x_hi * 2 + x_lo), y: 4, z: 8, core: 2. Of those that a mesh axis runs over, the one named last changes fastest.
Arguments:
- image_raw: bfloat16 [16384, 1152], P(('grp', 'blk')), may hold values from -1 to 1
- text_raw: bfloat16 [16384, 1152], P(('grp', 'blk')), may hold values from -1 to 1
- log_scale: float32 [1], replicated, may hold values from 1.6 to 2.6
- bias: float32 [1], replicated, may hold values from -5 to -2.5
Outputs:
- grad_image: bfloat16 [16384, 1152], P(('grp', 'blk'))
- grad_text: bfloat16 [16384, 1152], P(('grp', 'blk'))
The draws below stay inside these ranges and needn't reach their ends.
All inputs are finite; a program needn't handle non-finite values.
Results may differ from the reference program's by a relative error of at most 0.0069.
Values may be sent and summed in bfloat16 or wider, within the bound.
A program may use at most 64 MiB of HBM per device.

```python
import math
import jax
import jax.numpy as jnp
from jax import lax

D = 1152
BATCH = 16384


def shared_base(key):
    return jnp.clip(jax.random.normal(key, (BATCH, D), jnp.float32), -5.0, 5.0)


def row_scales(key):
    return jnp.exp(jax.random.uniform(key, (BATCH, 1), jnp.float32, math.log(0.3), math.log(3.0)))


def draw_image_raw(key, part):
    base = shared_base(key)
    key = jax.random.fold_in(key, 11)
    scales = row_scales(jax.random.fold_in(key, 1))
    values = base
    return jnp.clip(scales * values / math.sqrt(D), -1.0, 1.0).astype(jnp.bfloat16)


def draw_text_raw(key, part):
    base = shared_base(key)
    key = jax.random.fold_in(key, 23)
    scales = row_scales(jax.random.fold_in(key, 1))
    noise = jnp.clip(jax.random.normal(jax.random.fold_in(key, 2), (BATCH, D), jnp.float32), -5.0, 5.0)
    values = 0.6 * base + 0.8 * noise
    return jnp.clip(scales * values / math.sqrt(D), -1.0, 1.0).astype(jnp.bfloat16)


def setup_inputs(seed: int = 0) -> dict:
    splits = jax.random.split(jax.random.key(seed), 5)
    image_raw = draw_image_raw(jax.random.fold_in(splits[4], 71), 0)
    text_raw = draw_text_raw(jax.random.fold_in(splits[4], 71), 0)
    log_scale = jnp.clip(jax.random.uniform(splits[2], (1,), jnp.float32, 1.6, 2.6), 1.6, 2.6)
    bias = jnp.clip(jax.random.uniform(splits[3], (1,), jnp.float32, -5.0, -2.5), -5.0, -2.5)
    return dict(image_raw=image_raw, text_raw=text_raw, log_scale=log_scale, bias=bias)


def normalize(raw):
    values = raw.astype(jnp.float32)
    inverse = lax.rsqrt(lax.optimization_barrier(jnp.sum(values * values, axis=-1, keepdims=True)) + 1e-06)
    return (values * inverse, inverse)

def tangent(back, unit, inverse):
    along = lax.optimization_barrier(jnp.sum(unit * back, axis=-1, keepdims=True))
    return ((back - unit * along) * inverse).astype(jnp.bfloat16)

def reference(image_raw, text_raw, log_scale, bias):
    scale = jnp.exp(log_scale[0])
    offset = bias[0]
    image_unit, image_inv = normalize(image_raw)
    text_unit, text_inv = normalize(text_raw)
    image_half = image_unit.astype(jnp.bfloat16)
    text_half = text_unit.astype(jnp.bfloat16)
    total = image_raw.shape[0]
    width = image_raw.shape[1]
    step_rows = math.gcd(total, 512)
    count = total // step_rows
    blocks = image_half.reshape(count, step_rows, width)
    starts = jnp.arange(count, dtype=jnp.int32) * step_rows

    def visit(text_acc, item):
        block, start = item
        logits = scale * lax.dot_general(block.astype(jnp.float32), text_half.astype(jnp.float32), (((1,), (1,)), ((), ()))) + offset
        rows = lax.broadcasted_iota(jnp.int32, logits.shape, 0) + start
        cols = lax.broadcasted_iota(jnp.int32, logits.shape, 1)
        weight = (jax.nn.sigmoid(logits) - (rows == cols).astype(jnp.float32)).astype(jnp.bfloat16)
        image_back = scale * jnp.dot(weight, text_half, preferred_element_type=jnp.float32)
        text_add = lax.dot_general(weight.astype(jnp.float32), block.astype(jnp.float32), (((0,), (0,)), ((), ())))
        return (text_acc + scale * text_add, image_back)
    text_back, image_backs = lax.scan(visit, jnp.zeros((total, width), jnp.float32), (blocks, starts))
    image_back = image_backs.reshape(total, width)
    return (tangent(image_back, image_unit, image_inv), tangent(text_back, text_unit, text_inv))
```

```python
import functools

import jax
import jax.numpy as jnp
from jax import lax
from jax.experimental import pallas as pl
from jax.experimental.pallas import tpu as pltpu
from jax.sharding import PartitionSpec as P

NX, NY, NZ = 4, 4, 8
ROWS = 64
HALF = 32
QUARTER = 16
WIDTH = 1152
GROUP = 256
PLACE = {0: 0, 1: 1, 7: 2, 2: 3, 6: 4, 3: 5, 5: 6, 4: 7}


def coords():
    grp, blk = lax.axis_index("grp"), lax.axis_index("blk")
    core = lax.rem(grp, 2)
    y = lax.rem(grp // 2, NY)
    x = (blk // NZ) * 2 + grp // 8
    return x, y, lax.rem(blk, NZ), core


def device(x, y, z, core):
    x, y, z = lax.rem(x + NX, NX), lax.rem(y + NY, NY), lax.rem(z + NZ, NZ)
    return (lax.rem(x, 2) * 8 + y * 2 + core, (x // 2) * NZ + z)


def normalize(raw):
    values = raw.astype(jnp.float32)
    inverse = lax.rsqrt(jnp.sum(values * values, axis=-1, keepdims=True) + 1e-06)
    return values * inverse, inverse


def tangent(back, unit, inverse):
    along = jnp.sum(unit * back, axis=-1, keepdims=True)
    return ((back - unit * along) * inverse).astype(jnp.bfloat16)


def row_a(dy, dx):
    return dy * GROUP + dx * HALF


def row_b(dx, dy):
    return dx * GROUP + 128 + dy * HALF


def row_i(slot, other=0):
    return PLACE[slot] * 128 + other * ROWS


def kernel(image_ref, text_ref, scale_ref, bias_ref, out_image, out_text,
           images, texts, weight, text_sum, image_sum, text_send, pass_send, image_send, landing,
           send_sem, recv_sem):
    x, y, z, core = coords()
    near = {
        "x+": device(x + 1, y, z, core), "x-": device(x - 1, y, z, core),
        "y+": device(x, y + 1, z, core), "y-": device(x, y - 1, z, core),
        "z+": device(x, y, z + 1, core), "z-": device(x, y, z - 1, core),
        "c": device(x, y, z, 1 - core),
    }
    barrier = pltpu.get_barrier_semaphore()
    for target in near.values():
        pl.semaphore_signal(barrier, inc=1, device_id=target, device_id_type=pl.DeviceIdType.MESH)

    image_unit, _ = normalize(image_ref[...])
    images[pl.ds(0, ROWS), :] = image_unit.astype(jnp.bfloat16)
    text_unit, _ = normalize(text_ref[...])
    text_half = text_unit.astype(jnp.bfloat16)
    texts[pl.ds(row_a(0, 0), HALF), :] = text_half[:HALF]
    texts[pl.ds(row_b(0, 0), HALF), :] = text_half[HALF:]

    pl.semaphore_wait(barrier, len(near))

    copies = {}
    used = [0]

    def send(name, way, src, src_row, dst, dst_row, rows):
        number = len(copies)
        copy = pltpu.make_async_remote_copy(
            src_ref=src.at[pl.ds(src_row, rows)], dst_ref=dst.at[pl.ds(dst_row, rows)],
            send_sem=send_sem.at[number], recv_sem=recv_sem.at[number],
            device_id=near[way], device_id_type=pl.DeviceIdType.MESH,
        )
        copy.start()
        copies[name] = copy

    def arrived(name):
        copies[name].wait_recv()

    def text_hop(name, way, src, dst, rows=HALF):
        send(name, way, texts, src, texts, dst, rows)

    text_hop("ax1", "x+", row_a(0, 0), row_a(0, 1))
    text_hop("by1", "y+", row_b(0, 0), row_b(0, 1))
    text_hop("ax3", "x-", row_a(0, 0), row_a(0, 3))
    text_hop("by3", "y-", row_b(0, 0), row_b(0, 3))

    def image_hop(way, src, dst, part):
        send(f"i{dst}{part}", way, images, row_i(src) + part * HALF, images, row_i(dst) + part * HALF, HALF)

    def image_pass(slot):
        send(f"p{slot}", "c", images, row_i(slot), images, row_i(slot, 1), ROWS)

    for part in (0, 1):
        image_hop("z+", 0, 1, part)
        image_hop("z-", 0, 7, part)
    image_pass(0)

    def spread(k):
        text_hop(f"a1{k}", "y+", row_a(0, k), row_a(1, k))
        text_hop(f"b1{k}", "x+", row_b(0, k), row_b(1, k))
        text_hop(f"a3{k}", "y-", row_a(0, k), row_a(3, k))
        text_hop(f"b3{k}", "x-", row_b(0, k), row_b(3, k))

    spread(0)

    scale_row = jnp.exp(jnp.full((1, GROUP), scale_ref[0], jnp.float32))
    bias_row = jnp.full((1, GROUP), bias_ref[0], jnp.float32)

    def score(group, first, rows):
        block = texts[pl.ds(group * GROUP, GROUP), :]
        logits = lax.dot_general(
            images[pl.ds(first, rows), :], block, (((1,), (1,)), ((), ())), preferred_element_type=jnp.float32
        )
        value = 1.0 / (1.0 + jnp.exp(-(scale_row * logits + bias_row)))
        if group == 0 and first == 0:
            r = lax.broadcasted_iota(jnp.int32, logits.shape, 0)
            c = lax.broadcasted_iota(jnp.int32, logits.shape, 1)
            same = ((r < HALF) & (c == r)) | ((r >= HALF) & (r < ROWS) & (c == r + (128 - HALF)))
            value = value - same.astype(jnp.float32)
        weight[pl.ds(first, rows), pl.ds(group * GROUP, GROUP)] = value.astype(jnp.bfloat16)

    for name in ("ax1", "by1", "ax3", "by3"):
        arrived(name)
    text_hop("ax2p", "x+", row_a(0, 1), row_a(0, 2), QUARTER)
    text_hop("by2p", "y+", row_b(0, 1), row_b(0, 2), QUARTER)
    text_hop("ax2m", "x-", row_a(0, 3) + QUARTER, row_a(0, 2) + QUARTER, QUARTER)
    text_hop("by2m", "y-", row_b(0, 3) + QUARTER, row_b(0, 2) + QUARTER, QUARTER)
    spread(1)
    spread(3)
    for part in (0, 1):
        arrived(f"i1{part}")
        image_hop("z+", 1, 2, part)
        arrived(f"i7{part}")
        image_hop("z-", 7, 6, part)
    image_pass(1)
    image_pass(7)
    for name in ("a10", "b10", "a30", "b30"):
        arrived(name)
    text_hop("a20", "y+", row_a(1, 0), row_a(2, 0))
    text_hop("b20", "x+", row_b(1, 0), row_b(2, 0))
    for name in ("ax2p", "by2p", "ax2m", "by2m"):
        arrived(name)
    spread(2)
    for slot in (0, 1, 7):
        arrived(f"p{slot}")
    score(0, 0, 384)
    for part in (0, 1):
        arrived(f"i2{part}")
        image_hop("z+", 2, 3, part)
        arrived(f"i6{part}")
        image_hop("z-", 6, 5, part)
    image_pass(2)
    image_pass(6)
    for name in ("a11", "b11", "a31", "b31"):
        arrived(name)
    text_hop("a21", "y+", row_a(1, 1), row_a(2, 1))
    text_hop("b21", "x+", row_b(1, 1), row_b(2, 1))
    for name in ("a13", "b13", "a33", "b33"):
        arrived(name)
    text_hop("a23", "y-", row_a(3, 3), row_a(2, 3))
    text_hop("b23", "x-", row_b(3, 3), row_b(2, 3))
    for slot in (2, 6):
        arrived(f"p{slot}")
    score(0, 384, 256)
    for part in (0, 1):
        arrived(f"i3{part}")
        if part == 0:
            image_hop("z+", 3, 4, 0)
        arrived(f"i5{part}")
        if part == 1:
            image_hop("z-", 5, 4, 1)
    image_pass(3)
    image_pass(5)
    for name in ("a12", "b12", "a32", "b32"):
        arrived(name)
    text_hop("a22", "y-", row_a(3, 2), row_a(2, 2))
    text_hop("b22", "x-", row_b(3, 2), row_b(2, 2))
    for slot in (3, 5):
        arrived(f"p{slot}")
    score(0, 640, 256)
    score(1, 0, 896)
    score(3, 0, 896)
    arrived("i40")
    arrived("i41")
    image_pass(4)
    arrived("p4")
    for group in (0, 1, 3):
        score(group, 896, 128)
    for name in ("a20", "b20", "a21", "b21", "a23", "b23", "a22", "b22"):
        arrived(name)
    score(2, 0, 1024)

    landed = {}

    def scatter(name, way, src, src_row, rows):
        landed[name] = used[0]
        send(name, way, src, src_row, landing, used[0], rows)
        used[0] += rows

    def landing_of(name, rows, skip=0):
        return landing[pl.ds(landed[name] + skip, rows), :].astype(jnp.float32)

    def text_back(group):
        columns = pl.ds(group * GROUP, GROUP)
        return lax.dot_general(
            weight[:, columns], images[...], (((0,), (0,)), ((), ())), preferred_element_type=jnp.float32
        )

    def image_back(pair):
        return jnp.dot(
            weight[pl.ds(pair * GROUP, GROUP), :], texts[...], preferred_element_type=jnp.float32
        )

    def image_pair(pair, slots):
        back = image_back(pair)
        for n, slot in enumerate(slots):
            image_sum[pl.ds(pair * 128 + n * ROWS, ROWS), :] = back[n * 128:n * 128 + ROWS]
            pass_send[pl.ds(pair * 128 + n * ROWS, ROWS), :] = back[n * 128 + ROWS:(n + 1) * 128].astype(jnp.bfloat16)
            scatter(f"q{slot}", "c", pass_send, pair * 128 + n * ROWS, ROWS)

    def image_total(slot, skip=0, rows=ROWS):
        return image_sum[pl.ds(PLACE[slot] * ROWS + skip, rows), :] + landing_of(f"q{slot}", rows, skip)

    def image_on(slot, way, total):
        image_send[pl.ds(PLACE[slot] * ROWS, ROWS), :] = total.astype(jnp.bfloat16)
        scatter(f"j{slot}", way, image_send, PLACE[slot] * ROWS, ROWS)

    def text_on(name, way, row, total, skip=0, rows=HALF):
        text_send[pl.ds(row + skip, rows), :] = total.astype(jnp.bfloat16)
        scatter(name, way, text_send, row + skip, rows)

    text_send[pl.ds(2 * GROUP, GROUP), :] = text_back(2).astype(jnp.bfloat16)
    for k, way in ((2, "+"), (0, "-"), (3, "+"), (1, "-")):
        scatter(f"ta2{k}", "y" + way, text_send, row_a(2, k), HALF)
        scatter(f"tb2{k}", "x" + way, text_send, row_b(2, k), HALF)

    image_pair(3, (5, 4))
    arrived("q4")
    total = image_total(4)
    image_send[pl.ds(PLACE[4] * ROWS, ROWS), :] = total.astype(jnp.bfloat16)
    scatter("j4a", "z-", image_send, PLACE[4] * ROWS, HALF)
    scatter("j4b", "z+", image_send, PLACE[4] * ROWS + HALF, HALF)

    text_sum[pl.ds(1 * GROUP, GROUP), :] = text_back(1)
    for k in (2, 3):
        text_on(f"ta1{k}", "y-", row_a(1, k), text_sum[pl.ds(row_a(1, k), HALF), :])
        text_on(f"tb1{k}", "x-", row_b(1, k), text_sum[pl.ds(row_b(1, k), HALF), :])
    text_sum[pl.ds(3 * GROUP, GROUP), :] = text_back(3)
    for k in (1, 0):
        text_on(f"ta3{k}", "y+", row_a(3, k), text_sum[pl.ds(row_a(3, k), HALF), :])
        text_on(f"tb3{k}", "x+", row_b(3, k), text_sum[pl.ds(row_b(3, k), HALF), :])

    image_pair(2, (6, 3))
    arrived("q5")
    arrived("j4b")
    image_send[pl.ds(PLACE[5] * ROWS, HALF), :] = image_total(5, 0, HALF).astype(jnp.bfloat16)
    image_send[pl.ds(PLACE[5] * ROWS + HALF, HALF), :] = (
        image_total(5, HALF, HALF) + landing_of("j4b", HALF)
    ).astype(jnp.bfloat16)
    scatter("j5", "z+", image_send, PLACE[5] * ROWS, ROWS)
    arrived("q3")
    arrived("j4a")
    image_send[pl.ds(PLACE[3] * ROWS, HALF), :] = (
        image_total(3, 0, HALF) + landing_of("j4a", HALF)
    ).astype(jnp.bfloat16)
    image_send[pl.ds(PLACE[3] * ROWS + HALF, HALF), :] = image_total(3, HALF, HALF).astype(jnp.bfloat16)
    scatter("j3", "z-", image_send, PLACE[3] * ROWS, ROWS)

    for k, group, way in ((2, 3, "+"), (0, 1, "-"), (3, 3, "+"), (1, 1, "-")):
        arrived(f"ta2{k}")
        arrived(f"tb2{k}")
        text_on(f"ta{group}{k}", "y" + way, row_a(group, k),
                text_sum[pl.ds(row_a(group, k), HALF), :] + landing_of(f"ta2{k}", HALF))
        text_on(f"tb{group}{k}", "x" + way, row_b(group, k),
                text_sum[pl.ds(row_b(group, k), HALF), :] + landing_of(f"tb2{k}", HALF))

    image_pair(1, (7, 2))
    arrived("q6")
    arrived("j5")
    image_on(6, "z+", image_total(6) + landing_of("j5", ROWS))
    arrived("q2")
    arrived("j3")
    image_on(2, "z-", image_total(2) + landing_of("j3", ROWS))

    text_sum[pl.ds(0, GROUP), :] = text_back(0)

    def reduced(kind, k):
        arrived(f"t{kind}1{k}")
        arrived(f"t{kind}3{k}")
        row = (row_a if kind == "a" else row_b)(0, k)
        return (text_sum[pl.ds(row, HALF), :] + landing_of(f"t{kind}1{k}", HALF)) + landing_of(f"t{kind}3{k}", HALF)

    for kind, axis in (("a", "x"), ("b", "y")):
        row = (row_a if kind == "a" else row_b)(0, 2)
        text_send[pl.ds(row, HALF), :] = reduced(kind, 2).astype(jnp.bfloat16)
        scatter(f"u{kind}2m", axis + "-", text_send, row, QUARTER)
        scatter(f"u{kind}2p", axis + "+", text_send, row + QUARTER, QUARTER)

    image_pair(0, (0, 1))
    arrived("q7")
    arrived("j6")
    image_on(7, "z+", image_total(7) + landing_of("j6", ROWS))
    arrived("q1")
    arrived("j2")
    image_on(1, "z-", image_total(1) + landing_of("j2", ROWS))

    for k, part, way in ((1, "m", "-"), (3, "p", "+")):
        for kind, axis in (("a", "x"), ("b", "y")):
            row = (row_a if kind == "a" else row_b)(0, k)
            total = reduced(kind, k)
            arrived(f"u{kind}2{part}")
            extra = landing_of(f"u{kind}2{part}", QUARTER)
            if part == "m":
                total = jnp.concatenate([total[:QUARTER] + extra, total[QUARTER:]], axis=0)
            else:
                total = jnp.concatenate([total[:QUARTER], total[QUARTER:] + extra], axis=0)
            text_on(f"u{kind}{k}", axis + way, row, total)

    scale = jnp.exp(jnp.full((1, WIDTH), scale_ref[0], jnp.float32))
    image_unit, image_inv = normalize(image_ref[...])
    arrived("q0")
    arrived("j7")
    arrived("j1")
    back = (image_total(0) + landing_of("j7", ROWS)) + landing_of("j1", ROWS)
    out_image[...] = tangent(scale * back, image_unit, image_inv)

    text_unit, text_inv = normalize(text_ref[...])
    for n, kind in enumerate(("a", "b")):
        back = reduced(kind, 0)
        arrived(f"u{kind}1")
        arrived(f"u{kind}3")
        back = (back + landing_of(f"u{kind}1", HALF)) + landing_of(f"u{kind}3", HALF)
        part = slice(n * HALF, (n + 1) * HALF)
        out_text[pl.ds(n * HALF, HALF), :] = tangent(scale * back, text_unit[part], text_inv[part])

    for copy in copies.values():
        copy.wait_send()


COPIES = 120


def per_device(image_raw, text_raw, log_scale, bias):
    block = jax.ShapeDtypeStruct((ROWS, WIDTH), jnp.bfloat16)
    vmem = pl.BlockSpec(memory_space=pltpu.VMEM)
    smem = pl.BlockSpec(memory_space=pltpu.SMEM)
    half, full = jnp.bfloat16, jnp.float32
    return pl.pallas_call(
        kernel,
        out_shape=(block, block),
        in_specs=[vmem, vmem, smem, smem],
        out_specs=(vmem, vmem),
        scratch_shapes=[
            pltpu.VMEM((1024, WIDTH), half),
            pltpu.VMEM((1024, WIDTH), half),
            pltpu.VMEM((1024, 1024), half),
            pltpu.VMEM((1024, WIDTH), full),
            pltpu.VMEM((512, WIDTH), full),
            pltpu.VMEM((1024, WIDTH), half),
            pltpu.VMEM((512, WIDTH), half),
            pltpu.VMEM((512, WIDTH), half),
            pltpu.VMEM((2048, WIDTH), half),
            pltpu.SemaphoreType.DMA((COPIES,)),
            pltpu.SemaphoreType.DMA((COPIES,)),
        ],
        compiler_params=pltpu.CompilerParams(
            collective_id=0, has_side_effects=True, vmem_limit_bytes=52 * 2**20
        ),
        cost_estimate=pl.CostEstimate(flops=7_300_000_000, bytes_accessed=600_000, transcendentals=1_100_000),
    )(image_raw, text_raw, log_scale, bias)


def solution(mesh):
    rows = P(("grp", "blk"), None)
    return jax.shard_map(
        per_device, mesh=mesh, in_specs=(rows, rows, P(), P()), out_specs=(rows, rows), check_vma=False
    )
```

```python
import functools

import jax
import jax.numpy as jnp
from jax import lax
from jax.experimental import pallas as pl
from jax.experimental.pallas import tpu as pltpu
from jax.sharding import PartitionSpec as P

NX, NY, NZ = 4, 4, 8
ROWS = 64
HALF = 32
QUARTER = 16
WIDTH = 1152
GROUP = 256
PLACE = {0: 0, 1: 1, 7: 2, 2: 3, 6: 4, 3: 5, 5: 6, 4: 7}


def coords():
    grp, blk = lax.axis_index("grp"), lax.axis_index("blk")
    core = lax.rem(grp, 2)
    y = lax.rem(grp // 2, NY)
    x = (blk // NZ) * 2 + grp // 8
    return x, y, lax.rem(blk, NZ), core


def device(x, y, z, core):
    x, y, z = lax.rem(x + NX, NX), lax.rem(y + NY, NY), lax.rem(z + NZ, NZ)
    return (lax.rem(x, 2) * 8 + y * 2 + core, (x // 2) * NZ + z)


def normalize(raw):
    values = raw.astype(jnp.float32)
    inverse = lax.rsqrt(jnp.sum(values * values, axis=-1, keepdims=True) + 1e-06)
    return values * inverse, inverse


def tangent(back, unit, inverse):
    along = jnp.sum(unit * back, axis=-1, keepdims=True)
    return ((back - unit * along) * inverse).astype(jnp.bfloat16)


def row_a(dy, dx):
    return dy * GROUP + dx * HALF


def row_b(dx, dy):
    return dx * GROUP + 128 + dy * HALF


def row_i(slot, other=0):
    return PLACE[slot] * 128 + other * ROWS


def kernel(image_hbm, text_hbm, scale_ref, bias_ref, out_image, out_text,
           image_ref, text_ref, images, texts, weight, text_sum, image_sum, text_send, pass_send, image_send, landing,
           load_sem, send_sem, recv_sem):
    loads = [
        pltpu.make_async_copy(image_hbm, image_ref, load_sem.at[0]),
        pltpu.make_async_copy(text_hbm, text_ref, load_sem.at[1]),
    ]
    for load in loads:
        load.start()
    x, y, z, core = coords()
    near = {
        "x+": device(x + 1, y, z, core), "x-": device(x - 1, y, z, core),
        "y+": device(x, y + 1, z, core), "y-": device(x, y - 1, z, core),
        "z+": device(x, y, z + 1, core), "z-": device(x, y, z - 1, core),
        "c": device(x, y, z, 1 - core),
    }
    barrier = pltpu.get_barrier_semaphore()
    for target in near.values():
        pl.semaphore_signal(barrier, inc=1, device_id=target, device_id_type=pl.DeviceIdType.MESH)

    loads[0].wait()
    image_unit, _ = normalize(image_ref[...])
    images[pl.ds(0, ROWS), :] = image_unit.astype(jnp.bfloat16)
    loads[1].wait()
    text_unit, _ = normalize(text_ref[...])
    text_half = text_unit.astype(jnp.bfloat16)
    texts[pl.ds(row_a(0, 0), HALF), :] = text_half[:HALF]
    texts[pl.ds(row_b(0, 0), HALF), :] = text_half[HALF:]

    pl.semaphore_wait(barrier, len(near))

    copies = {}
    used = [0]

    def send(name, way, src, src_row, dst, dst_row, rows):
        number = len(copies)
        copy = pltpu.make_async_remote_copy(
            src_ref=src.at[pl.ds(src_row, rows)], dst_ref=dst.at[pl.ds(dst_row, rows)],
            send_sem=send_sem.at[number], recv_sem=recv_sem.at[number],
            device_id=near[way], device_id_type=pl.DeviceIdType.MESH,
        )
        copy.start()
        copies[name] = copy

    def arrived(*names):
        for name in names:
            copies[name].wait_recv()

    def text_hop(name, way, src, dst, rows=HALF):
        send(name, way, texts, src, texts, dst, rows)

    def first_hop(k, way, part):
        skip = part * QUARTER
        text_hop(f"ax{k}{part}", "x" + way, row_a(0, 0) + skip, row_a(0, k) + skip, QUARTER)
        text_hop(f"by{k}{part}", "y" + way, row_b(0, 0) + skip, row_b(0, k) + skip, QUARTER)

    def image_hop(way, src, dst, part):
        skip = part * QUARTER
        send(f"i{dst}{part}", way, images, row_i(src) + skip, images, row_i(dst) + skip, QUARTER)

    def image_pass(slot):
        send(f"p{slot}", "c", images, row_i(slot), images, row_i(slot, 1), ROWS)

    def image_step(hop, n):
        up, down = n, (n + 2) % 4
        if hop:
            arrived(f"i{hop}{up}", f"i{8 - hop}{down}")
        if hop < 3 or n < 2:
            image_hop("z+", hop, hop + 1, up)
            image_hop("z-", (8 - hop) % 8, 7 - hop, down)

    def spread(k):
        text_hop(f"a1{k}", "y+", row_a(0, k), row_a(1, k))
        text_hop(f"b1{k}", "x+", row_b(0, k), row_b(1, k))
        text_hop(f"a3{k}", "y-", row_a(0, k), row_a(3, k))
        text_hop(f"b3{k}", "x-", row_b(0, k), row_b(3, k))

    def forward(k, way, near_group):
        arrived(f"a{near_group}{k}", f"b{near_group}{k}")
        text_hop(f"a2{k}", "y" + way, row_a(near_group, k), row_a(2, k))
        text_hop(f"b2{k}", "x" + way, row_b(near_group, k), row_b(2, k))

    first_hop(1, "+", 0)
    first_hop(3, "-", 1)
    image_step(0, 0)
    first_hop(1, "+", 1)
    first_hop(3, "-", 0)
    image_step(0, 1)
    image_pass(0)
    spread(0)
    image_step(0, 2)
    image_step(0, 3)

    scale_row = jnp.exp(jnp.full((1, GROUP), scale_ref[0], jnp.float32))
    bias_row = jnp.full((1, GROUP), bias_ref[0], jnp.float32)

    def score(group, first, rows):
        block = texts[pl.ds(group * GROUP, GROUP), :]
        logits = lax.dot_general(
            images[pl.ds(first, rows), :], block, (((1,), (1,)), ((), ())), preferred_element_type=jnp.float32
        )
        value = 1.0 / (1.0 + jnp.exp(-(scale_row * logits + bias_row)))
        if group == 0 and first == 0:
            r = lax.broadcasted_iota(jnp.int32, logits.shape, 0)
            c = lax.broadcasted_iota(jnp.int32, logits.shape, 1)
            same = ((r < HALF) & (c == r)) | ((r >= HALF) & (r < ROWS) & (c == r + (128 - HALF)))
            value = value - same.astype(jnp.float32)
        weight[pl.ds(first, rows), pl.ds(group * GROUP, GROUP)] = value.astype(jnp.bfloat16)

    arrived("ax10", "by10", "ax31", "by31")
    text_hop("ax20", "x+", row_a(0, 1), row_a(0, 2), QUARTER)
    text_hop("by20", "y+", row_b(0, 1), row_b(0, 2), QUARTER)
    text_hop("ax21", "x-", row_a(0, 3) + QUARTER, row_a(0, 2) + QUARTER, QUARTER)
    text_hop("by21", "y-", row_b(0, 3) + QUARTER, row_b(0, 2) + QUARTER, QUARTER)
    image_step(1, 0)
    arrived("ax11", "by11", "ax30", "by30")
    spread(1)
    spread(3)
    image_step(1, 1)
    image_step(1, 2)
    image_step(1, 3)
    image_pass(1)
    image_pass(7)
    arrived("ax20", "by20", "ax21", "by21")
    spread(2)
    forward(0, "+", 1)
    image_step(2, 0)
    image_step(2, 1)
    arrived("p0", "p1", "p7")
    score(0, 0, 384)
    image_step(2, 2)
    forward(1, "+", 1)
    image_step(2, 3)
    image_pass(2)
    image_pass(6)
    image_step(3, 0)
    forward(3, "-", 3)
    image_step(3, 1)
    arrived("p2", "p6")
    score(0, 384, 256)
    forward(2, "-", 3)
    image_step(3, 2)
    image_step(3, 3)
    image_pass(3)
    image_pass(5)
    arrived("a30", "b30", "a31", "b31", "a12", "b12", "a13", "b13")
    score(1, 0, 640)
    arrived("i40", "i41", "i42", "i43")
    image_pass(4)
    score(3, 0, 640)
    arrived("p3", "p5", "p4")
    for group in (0, 1, 3):
        score(group, 640, 384)
    arrived("a20", "b20", "a21", "b21", "a23", "b23", "a22", "b22")
    score(2, 0, 1024)

    landed = {}

    def scatter(name, way, src, src_row, rows):
        landed[name] = used[0]
        send(name, way, src, src_row, landing, used[0], rows)
        used[0] += rows

    def landing_of(name, rows, skip=0):
        return landing[pl.ds(landed[name] + skip, rows), :].astype(jnp.float32)

    def text_back(group):
        columns = pl.ds(group * GROUP, GROUP)
        return lax.dot_general(
            weight[:, columns], images[...], (((0,), (0,)), ((), ())), preferred_element_type=jnp.float32
        )

    def image_back(pair):
        return jnp.dot(
            weight[pl.ds(pair * GROUP, GROUP), :], texts[...], preferred_element_type=jnp.float32
        )

    def image_pair(pair, slots):
        back = image_back(pair)
        for n, slot in enumerate(slots):
            image_sum[pl.ds(pair * 128 + n * ROWS, ROWS), :] = back[n * 128:n * 128 + ROWS]
            pass_send[pl.ds(pair * 128 + n * ROWS, ROWS), :] = back[n * 128 + ROWS:(n + 1) * 128].astype(jnp.bfloat16)
            scatter(f"q{slot}", "c", pass_send, pair * 128 + n * ROWS, ROWS)

    def image_on(slot, way, before, parts):
        for part in parts:
            row = PLACE[slot] * ROWS + part * QUARTER
            total = image_sum[pl.ds(row, QUARTER), :] + landing_of(f"q{slot}", QUARTER, part * QUARTER)
            if before is not None:
                arrived(f"j{before}{part}")
                total = total + landing_of(f"j{before}{part}", QUARTER)
            image_send[pl.ds(row, QUARTER), :] = total.astype(jnp.bfloat16)
            scatter(f"j{slot}{part}", way, image_send, row, QUARTER)

    def text_row(kind, group, k):
        return (row_a if kind == "a" else row_b)(group, k)

    def text_on(group, k, way, before=None):
        for kind, axis in (("a", "y"), ("b", "x")):
            row = text_row(kind, group, k)
            total = text_sum[pl.ds(row, HALF), :]
            if before is not None:
                arrived(f"t{kind}{before}{k}")
                total = total + landing_of(f"t{kind}{before}{k}", HALF)
            text_send[pl.ds(row, HALF), :] = total.astype(jnp.bfloat16)
            scatter(f"t{kind}{group}{k}", axis + way, text_send, row, HALF)

    def reduced(kind, k):
        arrived(f"t{kind}1{k}", f"t{kind}3{k}")
        total = text_sum[pl.ds(text_row(kind, 0, k), HALF), :]
        return (total + landing_of(f"t{kind}1{k}", HALF)) + landing_of(f"t{kind}3{k}", HALF)

    def second_far():
        for kind, axis in (("a", "x"), ("b", "y")):
            row = text_row(kind, 0, 2)
            text_send[pl.ds(row, HALF), :] = reduced(kind, 2).astype(jnp.bfloat16)
            scatter(f"u{kind}2m", axis + "-", text_send, row, QUARTER)
            scatter(f"u{kind}2p", axis + "+", text_send, row + QUARTER, QUARTER)

    def second_near(k, part, way):
        for kind, axis in (("a", "x"), ("b", "y")):
            row = text_row(kind, 0, k)
            total = reduced(kind, k)
            arrived(f"u{kind}2{part}")
            extra = landing_of(f"u{kind}2{part}", QUARTER)
            if part == "m":
                total = jnp.concatenate([total[:QUARTER] + extra, total[QUARTER:]], axis=0)
            else:
                total = jnp.concatenate([total[:QUARTER], total[QUARTER:] + extra], axis=0)
            text_send[pl.ds(row, HALF), :] = total.astype(jnp.bfloat16)
            scatter(f"u{kind}{k}", axis + way, text_send, row, HALF)

    image_pair(3, (5, 4))
    text_send[pl.ds(2 * GROUP, GROUP), :] = text_back(2).astype(jnp.bfloat16)
    for k, way in ((2, "+"), (1, "-"), (3, "+"), (0, "-")):
        scatter(f"ta2{k}", "y" + way, text_send, row_a(2, k), HALF)
        scatter(f"tb2{k}", "x" + way, text_send, row_b(2, k), HALF)
    arrived("q4", "q5")
    image_on(4, "z-", None, (0, 1))
    image_on(4, "z+", None, (2, 3))
    image_on(5, "z+", None, (0, 1))

    image_pair(2, (6, 3))
    text_sum[pl.ds(1 * GROUP, GROUP), :] = text_back(1)
    text_on(1, 2, "-")
    text_on(1, 3, "-")
    arrived("q3")
    image_on(3, "z-", None, (2, 3))
    text_sum[pl.ds(3 * GROUP, GROUP), :] = text_back(3)
    text_on(3, 1, "+")
    image_on(3, "z-", 4, (0, 1))
    image_on(5, "z+", 4, (2, 3))
    text_on(3, 2, "+", 2)
    text_on(1, 1, "-", 2)
    image_pair(1, (7, 2))
    arrived("q6")
    image_on(6, "z+", 5, (0, 1))
    text_on(3, 3, "+", 2)
    text_on(1, 0, "-", 2)
    text_on(3, 0, "+")
    arrived("q2")
    image_on(2, "z-", 3, (2, 3))
    image_on(6, "z+", 5, (2, 3))
    image_on(2, "z-", 3, (0, 1))
    text_sum[pl.ds(0, GROUP), :] = text_back(0)
    second_far()
    image_pair(0, (0, 1))
    arrived("q7")
    image_on(7, "z+", 6, (0, 1))
    arrived("q1")
    image_on(1, "z-", 2, (2, 3))
    image_on(7, "z+", 6, (2, 3))
    image_on(1, "z-", 2, (0, 1))
    second_near(1, "m", "-")
    second_near(3, "p", "+")

    scale = jnp.exp(jnp.full((1, WIDTH), scale_ref[0], jnp.float32))
    image_unit, image_inv = normalize(image_ref[...])
    arrived("q0")
    for part in range(4):
        arrived(f"j7{part}", f"j1{part}")
    up = jnp.concatenate([landing_of("j70", HALF), landing_of("j72", HALF)], axis=0)
    down = jnp.concatenate([landing_of("j10", HALF), landing_of("j12", HALF)], axis=0)
    back = (image_sum[pl.ds(0, ROWS), :] + landing_of("q0", ROWS)) + (up + down)
    out_image[...] = tangent(scale * back, image_unit, image_inv)

    text_unit, text_inv = normalize(text_ref[...])
    for n, kind in enumerate(("a", "b")):
        back = reduced(kind, 0)
        arrived(f"u{kind}1", f"u{kind}3")
        back = (back + landing_of(f"u{kind}1", HALF)) + landing_of(f"u{kind}3", HALF)
        part = slice(n * HALF, (n + 1) * HALF)
        out_text[pl.ds(n * HALF, HALF), :] = tangent(scale * back, text_unit[part], text_inv[part])

    for copy in copies.values():
        copy.wait_send()


COPIES = 144


def per_device(image_raw, text_raw, log_scale, bias):
    block = jax.ShapeDtypeStruct((ROWS, WIDTH), jnp.bfloat16)
    vmem = pl.BlockSpec(memory_space=pltpu.VMEM)
    smem = pl.BlockSpec(memory_space=pltpu.SMEM)
    hbm = pl.BlockSpec(memory_space=pl.ANY)
    half, full = jnp.bfloat16, jnp.float32
    return pl.pallas_call(
        kernel,
        out_shape=(block, block),
        in_specs=[hbm, hbm, smem, smem],
        out_specs=(vmem, vmem),
        scratch_shapes=[
            pltpu.VMEM((ROWS, WIDTH), half),
            pltpu.VMEM((ROWS, WIDTH), half),
            pltpu.VMEM((1024, WIDTH), half),
            pltpu.VMEM((1024, WIDTH), half),
            pltpu.VMEM((1024, 1024), half),
            pltpu.VMEM((1024, WIDTH), full),
            pltpu.VMEM((512, WIDTH), full),
            pltpu.VMEM((1024, WIDTH), half),
            pltpu.VMEM((512, WIDTH), half),
            pltpu.VMEM((512, WIDTH), half),
            pltpu.VMEM((2048, WIDTH), half),
            pltpu.SemaphoreType.DMA((2,)),
            pltpu.SemaphoreType.DMA((COPIES,)),
            pltpu.SemaphoreType.DMA((COPIES,)),
        ],
        compiler_params=pltpu.CompilerParams(
            collective_id=0, has_side_effects=True, vmem_limit_bytes=52 * 2**20
        ),
        cost_estimate=pl.CostEstimate(flops=7_300_000_000, bytes_accessed=600_000, transcendentals=1_100_000),
    )(image_raw, text_raw, log_scale, bias)


def solution(mesh):
    rows = P(("grp", "blk"), None)
    return jax.shard_map(
        per_device, mesh=mesh, in_specs=(rows, rows, P(), P()), out_specs=(rows, rows), check_vma=False
    )
```

```python
import functools

import jax
import jax.numpy as jnp
from jax import lax
from jax.experimental import pallas as pl
from jax.experimental.pallas import tpu as pltpu
from jax.sharding import PartitionSpec as P

NX, NY, NZ = 4, 4, 8
ROWS = 64
HALF = 32
QUARTER = 16
WIDTH = 1152
GROUP = 256
PLACE = {0: 0, 1: 1, 7: 2, 2: 3, 6: 4, 3: 5, 5: 6, 4: 7}


def coords():
    grp, blk = lax.axis_index("grp"), lax.axis_index("blk")
    core = lax.rem(grp, 2)
    y = lax.rem(grp // 2, NY)
    x = (blk // NZ) * 2 + grp // 8
    return x, y, lax.rem(blk, NZ), core


def device(x, y, z, core):
    x, y, z = lax.rem(x + NX, NX), lax.rem(y + NY, NY), lax.rem(z + NZ, NZ)
    return (lax.rem(x, 2) * 8 + y * 2 + core, (x // 2) * NZ + z)


def normalize(raw):
    values = raw.astype(jnp.float32)
    inverse = lax.rsqrt(jnp.sum(values * values, axis=-1, keepdims=True) + 1e-06)
    return values * inverse, inverse


def tangent(back, unit, inverse):
    along = jnp.sum(unit * back, axis=-1, keepdims=True)
    return ((back - unit * along) * inverse).astype(jnp.bfloat16)


def row_a(dy, dx):
    return dy * GROUP + dx * HALF


def row_b(dx, dy):
    return dx * GROUP + 128 + dy * HALF


def row_i(slot, other=0):
    return PLACE[slot] * 128 + other * ROWS


def kernel(image_ref, text_ref, scale_ref, bias_ref, out_image, out_text,
           images, texts, weight, text_sum, image_sum, text_send, pass_send, image_send, landing,
           send_sem, recv_sem):
    x, y, z, core = coords()
    near = {
        "x+": device(x + 1, y, z, core), "x-": device(x - 1, y, z, core),
        "y+": device(x, y + 1, z, core), "y-": device(x, y - 1, z, core),
        "z+": device(x, y, z + 1, core), "z-": device(x, y, z - 1, core),
        "c": device(x, y, z, 1 - core),
    }
    barrier = pltpu.get_barrier_semaphore()
    for target in near.values():
        pl.semaphore_signal(barrier, inc=1, device_id=target, device_id_type=pl.DeviceIdType.MESH)

    text_unit, _ = normalize(text_ref[...])
    text_half = text_unit.astype(jnp.bfloat16)
    texts[pl.ds(row_a(0, 0), HALF), :] = text_half[:HALF]
    texts[pl.ds(row_b(0, 0), HALF), :] = text_half[HALF:]
    image_unit, _ = normalize(image_ref[...])
    images[pl.ds(0, ROWS), :] = image_unit.astype(jnp.bfloat16)

    pl.semaphore_wait(barrier, len(near))

    copies = {}
    used = [0]

    def send(name, way, src, src_row, dst, dst_row, rows):
        number = len(copies)
        copy = pltpu.make_async_remote_copy(
            src_ref=src.at[pl.ds(src_row, rows)], dst_ref=dst.at[pl.ds(dst_row, rows)],
            send_sem=send_sem.at[number], recv_sem=recv_sem.at[number],
            device_id=near[way], device_id_type=pl.DeviceIdType.MESH,
        )
        copy.start()
        copies[name] = copy

    def arrived(*names):
        for name in names:
            copies[name].wait_recv()

    def text_hop(name, way, src, dst, rows=HALF):
        send(name, way, texts, src, texts, dst, rows)

    def first_hop(k, way, part):
        skip = part * QUARTER
        text_hop(f"ax{k}{part}", "x" + way, row_a(0, 0) + skip, row_a(0, k) + skip, QUARTER)
        text_hop(f"by{k}{part}", "y" + way, row_b(0, 0) + skip, row_b(0, k) + skip, QUARTER)

    def image_hop(way, src, dst, part):
        skip = part * QUARTER
        send(f"i{dst}{part}", way, images, row_i(src) + skip, images, row_i(dst) + skip, QUARTER)

    def image_pass(slot):
        send(f"p{slot}", "c", images, row_i(slot), images, row_i(slot, 1), ROWS)

    def image_step(hop, n):
        up, down = n, (n + 2) % 4
        if hop:
            arrived(f"i{hop}{up}", f"i{8 - hop}{down}")
        if hop < 3 or n < 2:
            image_hop("z+", hop, hop + 1, up)
            image_hop("z-", (8 - hop) % 8, 7 - hop, down)

    def spread(k):
        text_hop(f"a1{k}", "y+", row_a(0, k), row_a(1, k))
        text_hop(f"b1{k}", "x+", row_b(0, k), row_b(1, k))
        text_hop(f"a3{k}", "y-", row_a(0, k), row_a(3, k))
        text_hop(f"b3{k}", "x-", row_b(0, k), row_b(3, k))

    def forward(k, way, near_group):
        arrived(f"a{near_group}{k}", f"b{near_group}{k}")
        text_hop(f"a2{k}", "y" + way, row_a(near_group, k), row_a(2, k))
        text_hop(f"b2{k}", "x" + way, row_b(near_group, k), row_b(2, k))

    first_hop(1, "+", 0)
    first_hop(3, "-", 1)
    image_step(0, 0)
    first_hop(1, "+", 1)
    first_hop(3, "-", 0)
    image_step(0, 1)
    image_pass(0)
    spread(0)
    image_step(0, 2)
    image_step(0, 3)

    def score(first, rows, column, width):
        block = texts[pl.ds(column, width), :]
        logits = lax.dot_general(
            images[pl.ds(first, rows), :], block, (((1,), (1,)), ((), ())), preferred_element_type=jnp.float32
        )
        scale_row = jnp.exp(jnp.full((1, width), scale_ref[0], jnp.float32))
        value = 1.0 / (1.0 + jnp.exp(-(scale_row * logits + jnp.full((1, width), bias_ref[0], jnp.float32))))
        if column == 0 and first == 0:
            r = lax.broadcasted_iota(jnp.int32, logits.shape, 0)
            c = lax.broadcasted_iota(jnp.int32, logits.shape, 1)
            same = ((r < HALF) & (c == r)) | ((r >= HALF) & (r < ROWS) & (c == r + (128 - HALF)))
            value = value - same.astype(jnp.float32)
        weight[pl.ds(first, rows), pl.ds(column, width)] = value.astype(jnp.bfloat16)

    arrived("ax10", "by10", "ax31", "by31")
    text_hop("ax20", "x+", row_a(0, 1), row_a(0, 2), QUARTER)
    text_hop("by20", "y+", row_b(0, 1), row_b(0, 2), QUARTER)
    text_hop("ax21", "x-", row_a(0, 3) + QUARTER, row_a(0, 2) + QUARTER, QUARTER)
    text_hop("by21", "y-", row_b(0, 3) + QUARTER, row_b(0, 2) + QUARTER, QUARTER)
    image_step(1, 0)
    arrived("ax11", "by11", "ax30", "by30")
    spread(1)
    spread(3)
    image_step(1, 1)
    image_step(1, 2)
    image_step(1, 3)
    image_pass(1)
    image_pass(7)
    arrived("ax20", "by20", "ax21", "by21")
    spread(2)
    forward(0, "+", 1)
    image_step(2, 0)
    image_step(2, 1)
    arrived("p0", "p1", "p7")
    score(0, 384, 0, GROUP)
    image_step(2, 2)
    forward(1, "+", 1)
    image_step(2, 3)
    image_pass(2)
    image_pass(6)
    image_step(3, 0)
    forward(3, "-", 3)
    image_step(3, 1)
    forward(2, "-", 3)
    image_step(3, 2)
    image_step(3, 3)
    image_pass(3)
    image_pass(5)
    arrived("p2", "p6")
    score(384, 256, 0, GROUP)
    arrived("a30", "b30", "a31", "b31", "a12", "b12", "a13", "b13")
    score(0, 640, GROUP, GROUP)
    arrived("i40", "i41", "i42", "i43")
    image_pass(4)
    score(0, 640, 3 * GROUP, GROUP)
    arrived("p3", "p5")
    score(640, 256, 0, 2 * GROUP)
    score(640, 256, 3 * GROUP, GROUP)
    arrived("a20", "b20", "a21", "b21", "a23", "b23", "a22", "b22")
    score(0, 896, 2 * GROUP, GROUP)

    landed = {}

    def scatter(name, way, src, src_row, rows):
        landed[name] = used[0]
        send(name, way, src, src_row, landing, used[0], rows)
        used[0] += rows

    def landing_of(name, rows, skip=0):
        return landing[pl.ds(landed[name] + skip, rows), :].astype(jnp.float32)

    def text_back(group, first=0, rows=1024):
        return lax.dot_general(
            weight[pl.ds(first, rows), pl.ds(group * GROUP, GROUP)], images[pl.ds(first, rows), :],
            (((0,), (0,)), ((), ())), preferred_element_type=jnp.float32,
        )

    def image_back(*slots):
        back = jnp.dot(
            weight[pl.ds(row_i(slots[0]), 128 * len(slots)), :], texts[...], preferred_element_type=jnp.float32
        )
        for n, slot in enumerate(slots):
            place = PLACE[slot] * ROWS
            pass_send[pl.ds(place, ROWS), :] = back[n * 128 + ROWS:(n + 1) * 128].astype(jnp.bfloat16)
            scatter(f"q{slot}", "c", pass_send, place, ROWS)
            image_sum[pl.ds(place, ROWS), :] = back[n * 128:n * 128 + ROWS]

    def image_on(slot, way, before, parts):
        for part in parts:
            row = PLACE[slot] * ROWS + part * QUARTER
            total = image_sum[pl.ds(row, QUARTER), :] + landing_of(f"q{slot}", QUARTER, part * QUARTER)
            if before is not None:
                arrived(f"j{before}{part}")
                total = total + landing_of(f"j{before}{part}", QUARTER)
            image_send[pl.ds(row, QUARTER), :] = total.astype(jnp.bfloat16)
            scatter(f"j{slot}{part}", way, image_send, row, QUARTER)

    def text_row(kind, group, k):
        return (row_a if kind == "a" else row_b)(group, k)

    def text_on(group, k, way, before=None):
        for kind, axis in (("a", "y"), ("b", "x")):
            row = text_row(kind, group, k)
            total = text_sum[pl.ds(row, HALF), :]
            if before is not None:
                arrived(f"t{kind}{before}{k}")
                total = total + landing_of(f"t{kind}{before}{k}", HALF)
            text_send[pl.ds(row, HALF), :] = total.astype(jnp.bfloat16)
            scatter(f"t{kind}{group}{k}", axis + way, text_send, row, HALF)

    def reduced(kind, k):
        arrived(f"t{kind}1{k}", f"t{kind}3{k}")
        total = text_sum[pl.ds(text_row(kind, 0, k), HALF), :]
        return (total + landing_of(f"t{kind}1{k}", HALF)) + landing_of(f"t{kind}3{k}", HALF)

    def second_far():
        for kind, axis in (("a", "x"), ("b", "y")):
            row = text_row(kind, 0, 2)
            text_send[pl.ds(row, HALF), :] = reduced(kind, 2).astype(jnp.bfloat16)
            scatter(f"u{kind}2m", axis + "-", text_send, row, QUARTER)
            scatter(f"u{kind}2p", axis + "+", text_send, row + QUARTER, QUARTER)

    def second_near(k, part, way):
        for kind, axis in (("a", "x"), ("b", "y")):
            row = text_row(kind, 0, k)
            total = reduced(kind, k)
            arrived(f"u{kind}2{part}")
            extra = landing_of(f"u{kind}2{part}", QUARTER)
            if part == "m":
                total = jnp.concatenate([total[:QUARTER] + extra, total[QUARTER:]], axis=0)
            else:
                total = jnp.concatenate([total[:QUARTER], total[QUARTER:] + extra], axis=0)
            text_send[pl.ds(row, HALF), :] = total.astype(jnp.bfloat16)
            scatter(f"u{kind}{k}", axis + way, text_send, row, HALF)

    def far_on(k, way):
        scatter(f"ta2{k}", "y" + way, text_send, row_a(2, k), HALF)
        scatter(f"tb2{k}", "x" + way, text_send, row_b(2, k), HALF)

    arrived("p4")
    score(896, 128, 0, 4 * GROUP)
    text_send[pl.ds(2 * GROUP, GROUP), :] = text_back(2).astype(jnp.bfloat16)
    far_on(2, "+")
    far_on(1, "-")
    far_on(3, "+")
    image_back(4)
    image_back(3, 5)
    text_sum[pl.ds(1 * GROUP, GROUP), :] = text_back(1)
    text_on(1, 2, "-")
    far_on(0, "-")
    arrived("q4")
    image_on(4, "z-", None, (0, 1))
    image_on(4, "z+", None, (2, 3))
    text_sum[pl.ds(3 * GROUP, GROUP), :] = text_back(3)
    arrived("q3", "q5")
    image_on(3, "z-", None, (2, 3))
    image_on(5, "z+", None, (0, 1))
    text_on(3, 2, "+", 2)
    text_on(3, 1, "+")
    text_on(1, 1, "-", 2)
    text_on(1, 3, "-")
    image_back(2, 6)
    image_on(3, "z-", 4, (0, 1))
    image_on(5, "z+", 4, (2, 3))
    text_on(3, 3, "+", 2)
    text_sum[pl.ds(0, GROUP), :] = text_back(0)
    arrived("q2", "q6")
    image_on(2, "z-", 3, (2, 3))
    image_on(6, "z+", 5, (0, 1))
    image_back(1, 7)
    second_far()
    image_on(2, "z-", 3, (0, 1))
    image_on(6, "z+", 5, (2, 3))
    text_on(1, 0, "-", 2)
    text_on(3, 0, "+")
    image_back(0)
    arrived("q1", "q7")
    image_on(1, "z-", 2, (2, 3))
    image_on(7, "z+", 6, (0, 1))
    second_near(1, "m", "-")
    second_near(3, "p", "+")
    image_on(1, "z-", 2, (0, 1))
    image_on(7, "z+", 6, (2, 3))

    scale = jnp.exp(jnp.full((1, WIDTH), scale_ref[0], jnp.float32))
    image_unit, image_inv = normalize(image_ref[...])
    arrived("q0")
    for part in range(4):
        arrived(f"j7{part}", f"j1{part}")
    up = jnp.concatenate([landing_of("j70", HALF), landing_of("j72", HALF)], axis=0)
    down = jnp.concatenate([landing_of("j10", HALF), landing_of("j12", HALF)], axis=0)
    back = (image_sum[pl.ds(0, ROWS), :] + landing_of("q0", ROWS)) + (up + down)
    out_image[...] = tangent(scale * back, image_unit, image_inv)

    text_unit, text_inv = normalize(text_ref[...])
    for n, kind in enumerate(("a", "b")):
        back = reduced(kind, 0)
        arrived(f"u{kind}1", f"u{kind}3")
        back = (back + landing_of(f"u{kind}1", HALF)) + landing_of(f"u{kind}3", HALF)
        part = slice(n * HALF, (n + 1) * HALF)
        out_text[pl.ds(n * HALF, HALF), :] = tangent(scale * back, text_unit[part], text_inv[part])

    for copy in copies.values():
        copy.wait_send()


COPIES = 144


def per_device(image_raw, text_raw, log_scale, bias):
    block = jax.ShapeDtypeStruct((ROWS, WIDTH), jnp.bfloat16)
    vmem = pl.BlockSpec(memory_space=pltpu.VMEM)
    smem = pl.BlockSpec(memory_space=pltpu.SMEM)
    half, full = jnp.bfloat16, jnp.float32
    return pl.pallas_call(
        kernel,
        out_shape=(block, block),
        in_specs=[vmem, vmem, smem, smem],
        out_specs=(vmem, vmem),
        scratch_shapes=[
            pltpu.VMEM((1024, WIDTH), half),
            pltpu.VMEM((1024, WIDTH), half),
            pltpu.VMEM((1024, 1024), half),
            pltpu.VMEM((1024, WIDTH), full),
            pltpu.VMEM((512, WIDTH), full),
            pltpu.VMEM((1024, WIDTH), half),
            pltpu.VMEM((512, WIDTH), half),
            pltpu.VMEM((512, WIDTH), half),
            pltpu.VMEM((2048, WIDTH), half),
            pltpu.SemaphoreType.DMA((COPIES,)),
            pltpu.SemaphoreType.DMA((COPIES,)),
        ],
        compiler_params=pltpu.CompilerParams(
            collective_id=0, has_side_effects=True, vmem_limit_bytes=52 * 2**20
        ),
        cost_estimate=pl.CostEstimate(flops=7_300_000_000, bytes_accessed=600_000, transcendentals=1_100_000),
    )(image_raw, text_raw, log_scale, bias)


def solution(mesh):
    rows = P(("grp", "blk"), None)
    return jax.shard_map(
        per_device, mesh=mesh, in_specs=(rows, rows, P(), P()), out_specs=(rows, rows), check_vma=False
    )
```

```python
import functools

import jax
import jax.numpy as jnp
from jax import lax
from jax.experimental import pallas as pl
from jax.experimental.pallas import tpu as pltpu
from jax.sharding import PartitionSpec as P

NX, NY, NZ = 4, 4, 8
ROWS = 64
HALF = 32
QUARTER = 16
WIDTH = 1152
GROUP = 256
PLACE = {0: 0, 1: 1, 7: 2, 2: 3, 6: 4, 3: 5, 5: 6, 4: 7}


def coords():
    grp, blk = lax.axis_index("grp"), lax.axis_index("blk")
    core = lax.rem(grp, 2)
    y = lax.rem(grp // 2, NY)
    x = (blk // NZ) * 2 + grp // 8
    return x, y, lax.rem(blk, NZ), core


def device(x, y, z, core):
    x, y, z = lax.rem(x + NX, NX), lax.rem(y + NY, NY), lax.rem(z + NZ, NZ)
    return (lax.rem(x, 2) * 8 + y * 2 + core, (x // 2) * NZ + z)


def normalize(raw):
    values = raw.astype(jnp.float32)
    inverse = lax.rsqrt(jnp.sum(values * values, axis=-1, keepdims=True) + 1e-06)
    return values * inverse, inverse


def tangent(back, unit, inverse):
    along = jnp.sum(unit * back, axis=-1, keepdims=True)
    return ((back - unit * along) * inverse).astype(jnp.bfloat16)


def row_a(dy, dx):
    return dy * GROUP + dx * HALF


def row_b(dx, dy):
    return dx * GROUP + 128 + dy * HALF


def row_i(slot, other=0):
    return PLACE[slot] * 128 + other * ROWS


def kernel(raw_ref, scale_ref, bias_ref, out,
           images, texts, weight, text_sum, image_sum, text_send, pass_send, image_send, landing,
           send_sem, recv_sem):
    image_ref, text_ref = raw_ref.at[pl.ds(0, ROWS)], raw_ref.at[pl.ds(ROWS, ROWS)]
    x, y, z, core = coords()
    near = {
        "x+": device(x + 1, y, z, core), "x-": device(x - 1, y, z, core),
        "y+": device(x, y + 1, z, core), "y-": device(x, y - 1, z, core),
        "z+": device(x, y, z + 1, core), "z-": device(x, y, z - 1, core),
        "c": device(x, y, z, 1 - core),
    }
    barrier = pltpu.get_barrier_semaphore()
    for target in near.values():
        pl.semaphore_signal(barrier, inc=1, device_id=target, device_id_type=pl.DeviceIdType.MESH)

    text_unit, _ = normalize(text_ref[...])
    text_half = text_unit.astype(jnp.bfloat16)
    texts[pl.ds(row_a(0, 0), HALF), :] = text_half[:HALF]
    texts[pl.ds(row_b(0, 0), HALF), :] = text_half[HALF:]
    image_unit, _ = normalize(image_ref[...])
    images[pl.ds(0, ROWS), :] = image_unit.astype(jnp.bfloat16)

    pl.semaphore_wait(barrier, len(near))

    copies = {}
    used = [0]

    def send(name, way, src, src_row, dst, dst_row, rows):
        number = len(copies)
        copy = pltpu.make_async_remote_copy(
            src_ref=src.at[pl.ds(src_row, rows)], dst_ref=dst.at[pl.ds(dst_row, rows)],
            send_sem=send_sem.at[number], recv_sem=recv_sem.at[number],
            device_id=near[way], device_id_type=pl.DeviceIdType.MESH,
        )
        copy.start()
        copies[name] = copy

    def arrived(*names):
        for name in names:
            copies[name].wait_recv()

    def text_hop(name, way, src, dst, rows=HALF):
        send(name, way, texts, src, texts, dst, rows)

    def first_hop(k, way, part):
        skip = part * QUARTER
        text_hop(f"ax{k}{part}", "x" + way, row_a(0, 0) + skip, row_a(0, k) + skip, QUARTER)
        text_hop(f"by{k}{part}", "y" + way, row_b(0, 0) + skip, row_b(0, k) + skip, QUARTER)

    def image_hop(way, src, dst, part):
        skip = part * QUARTER
        send(f"i{dst}{part}", way, images, row_i(src) + skip, images, row_i(dst) + skip, QUARTER)

    def image_pass(slot):
        send(f"p{slot}", "c", images, row_i(slot), images, row_i(slot, 1), ROWS)

    def image_step(hop, n):
        up, down = n, (n + 2) % 4
        if hop:
            arrived(f"i{hop}{up}", f"i{8 - hop}{down}")
        if hop < 3 or n < 2:
            image_hop("z+", hop, hop + 1, up)
            image_hop("z-", (8 - hop) % 8, 7 - hop, down)

    def spread(k):
        text_hop(f"a1{k}", "y+", row_a(0, k), row_a(1, k))
        text_hop(f"b1{k}", "x+", row_b(0, k), row_b(1, k))
        text_hop(f"a3{k}", "y-", row_a(0, k), row_a(3, k))
        text_hop(f"b3{k}", "x-", row_b(0, k), row_b(3, k))

    def forward(k, way, near_group):
        arrived(f"a{near_group}{k}", f"b{near_group}{k}")
        text_hop(f"a2{k}", "y" + way, row_a(near_group, k), row_a(2, k))
        text_hop(f"b2{k}", "x" + way, row_b(near_group, k), row_b(2, k))

    first_hop(1, "+", 0)
    first_hop(3, "-", 1)
    image_step(0, 0)
    first_hop(1, "+", 1)
    first_hop(3, "-", 0)
    image_step(0, 1)
    image_pass(0)
    spread(0)
    image_step(0, 2)
    image_step(0, 3)

    def score(first, rows, column, width):
        block = texts[pl.ds(column, width), :]
        logits = lax.dot_general(
            images[pl.ds(first, rows), :], block, (((1,), (1,)), ((), ())), preferred_element_type=jnp.float32
        )
        scale_row = jnp.exp(jnp.full((1, width), scale_ref[0], jnp.float32))
        value = 1.0 / (1.0 + jnp.exp(-(scale_row * logits + jnp.full((1, width), bias_ref[0], jnp.float32))))
        if column == 0 and first == 0:
            r = lax.broadcasted_iota(jnp.int32, logits.shape, 0)
            c = lax.broadcasted_iota(jnp.int32, logits.shape, 1)
            same = ((r < HALF) & (c == r)) | ((r >= HALF) & (r < ROWS) & (c == r + (128 - HALF)))
            value = value - same.astype(jnp.float32)
        weight[pl.ds(first, rows), pl.ds(column, width)] = value.astype(jnp.bfloat16)

    arrived("ax10", "by10", "ax31", "by31")
    text_hop("ax20", "x+", row_a(0, 1), row_a(0, 2), QUARTER)
    text_hop("by20", "y+", row_b(0, 1), row_b(0, 2), QUARTER)
    text_hop("ax21", "x-", row_a(0, 3) + QUARTER, row_a(0, 2) + QUARTER, QUARTER)
    text_hop("by21", "y-", row_b(0, 3) + QUARTER, row_b(0, 2) + QUARTER, QUARTER)
    image_step(1, 0)
    arrived("ax11", "by11", "ax30", "by30")
    spread(1)
    spread(3)
    image_step(1, 1)
    image_step(1, 2)
    image_step(1, 3)
    image_pass(1)
    image_pass(7)
    arrived("ax20", "by20", "ax21", "by21")
    spread(2)
    forward(0, "+", 1)
    image_step(2, 0)
    image_step(2, 1)
    arrived("p0", "p1", "p7")
    score(0, 384, 0, GROUP)
    image_step(2, 2)
    forward(1, "+", 1)
    image_step(2, 3)
    image_pass(2)
    image_pass(6)
    image_step(3, 0)
    forward(3, "-", 3)
    image_step(3, 1)
    forward(2, "-", 3)
    image_step(3, 2)
    image_step(3, 3)
    image_pass(3)
    image_pass(5)
    arrived("p2", "p6")
    score(384, 256, 0, GROUP)
    arrived("a30", "b30", "a31", "b31", "a12", "b12", "a13", "b13")
    score(0, 640, GROUP, GROUP)
    arrived("i40", "i41", "i42", "i43")
    image_pass(4)
    score(0, 640, 3 * GROUP, GROUP)
    arrived("p3", "p5")
    score(640, 256, 0, 2 * GROUP)
    score(640, 256, 3 * GROUP, GROUP)
    arrived("a20", "b20", "a21", "b21", "a23", "b23", "a22", "b22")
    score(0, 896, 2 * GROUP, GROUP)

    landed = {}

    def scatter(name, way, src, src_row, rows):
        landed[name] = used[0]
        send(name, way, src, src_row, landing, used[0], rows)
        used[0] += rows

    def landing_of(name, rows, skip=0):
        return landing[pl.ds(landed[name] + skip, rows), :].astype(jnp.float32)

    def text_back(group, first=0, rows=1024):
        return lax.dot_general(
            weight[pl.ds(first, rows), pl.ds(group * GROUP, GROUP)], images[pl.ds(first, rows), :],
            (((0,), (0,)), ((), ())), preferred_element_type=jnp.float32,
        )

    def image_back(*slots):
        back = jnp.dot(
            weight[pl.ds(row_i(slots[0]), 128 * len(slots)), :], texts[...], preferred_element_type=jnp.float32
        )
        for n, slot in enumerate(slots):
            place = PLACE[slot] * ROWS
            pass_send[pl.ds(place, ROWS), :] = back[n * 128 + ROWS:(n + 1) * 128].astype(jnp.bfloat16)
            scatter(f"q{slot}", "c", pass_send, place, ROWS)
            image_sum[pl.ds(place, ROWS), :] = back[n * 128:n * 128 + ROWS]

    def image_on(slot, way, before, parts):
        for part in parts:
            row = PLACE[slot] * ROWS + part * QUARTER
            total = image_sum[pl.ds(row, QUARTER), :] + landing_of(f"q{slot}", QUARTER, part * QUARTER)
            if before is not None:
                arrived(f"j{before}{part}")
                total = total + landing_of(f"j{before}{part}", QUARTER)
            image_send[pl.ds(row, QUARTER), :] = total.astype(jnp.bfloat16)
            scatter(f"j{slot}{part}", way, image_send, row, QUARTER)

    def text_row(kind, group, k):
        return (row_a if kind == "a" else row_b)(group, k)

    def text_on(group, k, way, before=None):
        for kind, axis in (("a", "y"), ("b", "x")):
            row = text_row(kind, group, k)
            total = text_sum[pl.ds(row, HALF), :]
            if before is not None:
                arrived(f"t{kind}{before}{k}")
                total = total + landing_of(f"t{kind}{before}{k}", HALF)
            text_send[pl.ds(row, HALF), :] = total.astype(jnp.bfloat16)
            scatter(f"t{kind}{group}{k}", axis + way, text_send, row, HALF)

    def reduced(kind, k):
        arrived(f"t{kind}1{k}", f"t{kind}3{k}")
        total = text_sum[pl.ds(text_row(kind, 0, k), HALF), :]
        return (total + landing_of(f"t{kind}1{k}", HALF)) + landing_of(f"t{kind}3{k}", HALF)

    def second_far():
        for kind, axis in (("a", "x"), ("b", "y")):
            row = text_row(kind, 0, 2)
            text_send[pl.ds(row, HALF), :] = reduced(kind, 2).astype(jnp.bfloat16)
            scatter(f"u{kind}2m", axis + "-", text_send, row, QUARTER)
            scatter(f"u{kind}2p", axis + "+", text_send, row + QUARTER, QUARTER)

    def second_near(k, part, way):
        for kind, axis in (("a", "x"), ("b", "y")):
            row = text_row(kind, 0, k)
            total = reduced(kind, k)
            arrived(f"u{kind}2{part}")
            extra = landing_of(f"u{kind}2{part}", QUARTER)
            if part == "m":
                total = jnp.concatenate([total[:QUARTER] + extra, total[QUARTER:]], axis=0)
            else:
                total = jnp.concatenate([total[:QUARTER], total[QUARTER:] + extra], axis=0)
            text_send[pl.ds(row, HALF), :] = total.astype(jnp.bfloat16)
            scatter(f"u{kind}{k}", axis + way, text_send, row, HALF)

    def far_on(k, way):
        scatter(f"ta2{k}", "y" + way, text_send, row_a(2, k), HALF)
        scatter(f"tb2{k}", "x" + way, text_send, row_b(2, k), HALF)

    arrived("p4")
    score(896, 128, 0, 4 * GROUP)
    text_send[pl.ds(2 * GROUP, GROUP), :] = text_back(2).astype(jnp.bfloat16)
    far_on(2, "+")
    far_on(1, "-")
    far_on(3, "+")
    image_back(4)
    image_back(3, 5)
    text_sum[pl.ds(1 * GROUP, GROUP), :] = text_back(1)
    text_on(1, 2, "-")
    far_on(0, "-")
    arrived("q4")
    image_on(4, "z-", None, (0, 1))
    image_on(4, "z+", None, (2, 3))
    text_sum[pl.ds(3 * GROUP, GROUP), :] = text_back(3)
    arrived("q3", "q5")
    image_on(3, "z-", None, (2, 3))
    image_on(5, "z+", None, (0, 1))
    text_on(3, 2, "+", 2)
    text_on(3, 1, "+")
    text_on(1, 1, "-", 2)
    text_on(1, 3, "-")
    image_back(2, 6)
    image_on(3, "z-", 4, (0, 1))
    image_on(5, "z+", 4, (2, 3))
    text_on(3, 3, "+", 2)
    text_sum[pl.ds(0, GROUP), :] = text_back(0)
    arrived("q2", "q6")
    image_on(2, "z-", 3, (2, 3))
    image_on(6, "z+", 5, (0, 1))
    image_back(1, 7)
    second_far()
    image_on(2, "z-", 3, (0, 1))
    image_on(6, "z+", 5, (2, 3))
    text_on(1, 0, "-", 2)
    text_on(3, 0, "+")
    image_back(0)
    arrived("q1", "q7")
    image_on(1, "z-", 2, (2, 3))
    image_on(7, "z+", 6, (0, 1))
    second_near(1, "m", "-")
    second_near(3, "p", "+")
    image_on(1, "z-", 2, (0, 1))
    image_on(7, "z+", 6, (2, 3))

    scale = jnp.exp(jnp.full((1, WIDTH), scale_ref[0], jnp.float32))
    image_unit, image_inv = normalize(image_ref[...])
    arrived("q0")
    for part in range(4):
        arrived(f"j7{part}", f"j1{part}")
    up = jnp.concatenate([landing_of("j70", HALF), landing_of("j72", HALF)], axis=0)
    down = jnp.concatenate([landing_of("j10", HALF), landing_of("j12", HALF)], axis=0)
    back = (image_sum[pl.ds(0, ROWS), :] + landing_of("q0", ROWS)) + (up + down)
    out[pl.ds(0, ROWS), :] = tangent(scale * back, image_unit, image_inv)

    text_unit, text_inv = normalize(text_ref[...])
    for n, kind in enumerate(("a", "b")):
        back = reduced(kind, 0)
        arrived(f"u{kind}1", f"u{kind}3")
        back = (back + landing_of(f"u{kind}1", HALF)) + landing_of(f"u{kind}3", HALF)
        part = slice(n * HALF, (n + 1) * HALF)
        out[pl.ds(ROWS + n * HALF, HALF), :] = tangent(scale * back, text_unit[part], text_inv[part])

    for copy in copies.values():
        copy.wait_send()


COPIES = 144


def per_device(image_raw, text_raw, log_scale, bias):
    block = jax.ShapeDtypeStruct((2 * ROWS, WIDTH), jnp.bfloat16)
    vmem = pl.BlockSpec(memory_space=pltpu.VMEM)
    smem = pl.BlockSpec(memory_space=pltpu.SMEM)
    half, full = jnp.bfloat16, jnp.float32
    both = pl.pallas_call(
        kernel,
        out_shape=block,
        in_specs=[vmem, smem, smem],
        out_specs=vmem,
        scratch_shapes=[
            pltpu.VMEM((1024, WIDTH), half),
            pltpu.VMEM((1024, WIDTH), half),
            pltpu.VMEM((1024, 1024), half),
            pltpu.VMEM((1024, WIDTH), full),
            pltpu.VMEM((512, WIDTH), full),
            pltpu.VMEM((1024, WIDTH), half),
            pltpu.VMEM((512, WIDTH), half),
            pltpu.VMEM((512, WIDTH), half),
            pltpu.VMEM((2048, WIDTH), half),
            pltpu.SemaphoreType.DMA((COPIES,)),
            pltpu.SemaphoreType.DMA((COPIES,)),
        ],
        compiler_params=pltpu.CompilerParams(
            collective_id=0, has_side_effects=True, vmem_limit_bytes=52 * 2**20
        ),
        cost_estimate=pl.CostEstimate(flops=7_300_000_000, bytes_accessed=600_000, transcendentals=1_100_000),
    )(jnp.concatenate([image_raw, text_raw], axis=0), log_scale, bias)
    return both[:ROWS], both[ROWS:]


def solution(mesh):
    rows = P(("grp", "blk"), None)
    return jax.shard_map(
        per_device, mesh=mesh, in_specs=(rows, rows, P(), P()), out_specs=(rows, rows), check_vma=False
    )
```

```python
import functools

import jax
import jax.numpy as jnp
from jax import lax
from jax.experimental import pallas as pl
from jax.experimental.pallas import tpu as pltpu
from jax.sharding import PartitionSpec as P

NX, NY, NZ = 4, 4, 8
ROWS = 64
HALF = 32
QUARTER = 16
WIDTH = 1152
GROUP = 256
PLACE = {0: 0, 1: 1, 7: 2, 2: 3, 6: 4, 3: 5, 5: 6, 4: 7}


def coords():
    grp, blk = lax.axis_index("grp"), lax.axis_index("blk")
    core = lax.rem(grp, 2)
    y = lax.rem(grp // 2, NY)
    x = (blk // NZ) * 2 + grp // 8
    return x, y, lax.rem(blk, NZ), core


def device(x, y, z, core):
    x, y, z = lax.rem(x + NX, NX), lax.rem(y + NY, NY), lax.rem(z + NZ, NZ)
    return (lax.rem(x, 2) * 8 + y * 2 + core, (x // 2) * NZ + z)


def normalize(raw):
    values = raw.astype(jnp.float32)
    inverse = lax.rsqrt(jnp.sum(values * values, axis=-1, keepdims=True) + 1e-06)
    return values * inverse, inverse


def tangent(back, unit, inverse):
    along = jnp.sum(unit * back, axis=-1, keepdims=True)
    return ((back - unit * along) * inverse).astype(jnp.bfloat16)


def text_place(group, k):
    if group in (0, 2):
        return group // 2 * 3 * GROUP + k * HALF
    return (GROUP if k < 2 else 2 * GROUP) + group // 2 * ROWS + k % 2 * HALF


def row_a(dy, dx):
    return text_place(dy, dx)


def row_b(dx, dy):
    return text_place(dx, dy) + 128


def row_i(slot, other=0):
    return PLACE[slot] * 128 + other * ROWS


def kernel(raw_ref, scale_ref, bias_ref, out,
           images, texts, weight, text_sum, image_sum, text_send, pass_send, image_send, landing,
           send_sem, recv_sem):
    image_ref, text_ref = raw_ref.at[pl.ds(0, ROWS)], raw_ref.at[pl.ds(ROWS, ROWS)]
    x, y, z, core = coords()
    near = {
        "x+": device(x + 1, y, z, core), "x-": device(x - 1, y, z, core),
        "y+": device(x, y + 1, z, core), "y-": device(x, y - 1, z, core),
        "z+": device(x, y, z + 1, core), "z-": device(x, y, z - 1, core),
        "c": device(x, y, z, 1 - core),
    }
    barrier = pltpu.get_barrier_semaphore()
    for target in near.values():
        pl.semaphore_signal(barrier, inc=1, device_id=target, device_id_type=pl.DeviceIdType.MESH)

    text_unit, _ = normalize(text_ref[...])
    text_half = text_unit.astype(jnp.bfloat16)
    texts[pl.ds(row_a(0, 0), HALF), :] = text_half[:HALF]
    texts[pl.ds(row_b(0, 0), HALF), :] = text_half[HALF:]
    image_unit, _ = normalize(image_ref[...])
    images[pl.ds(0, ROWS), :] = image_unit.astype(jnp.bfloat16)

    pl.semaphore_wait(barrier, len(near))

    copies = {}
    used = [0]

    def send(name, way, src, src_row, dst, dst_row, rows):
        number = len(copies)
        copy = pltpu.make_async_remote_copy(
            src_ref=src.at[pl.ds(src_row, rows)], dst_ref=dst.at[pl.ds(dst_row, rows)],
            send_sem=send_sem.at[number], recv_sem=recv_sem.at[number],
            device_id=near[way], device_id_type=pl.DeviceIdType.MESH,
        )
        copy.start()
        copies[name] = copy

    def arrived(*names):
        for name in names:
            copies[name].wait_recv()

    def text_hop(name, way, src, dst, rows=HALF):
        send(name, way, texts, src, texts, dst, rows)

    def first_hop(k, way, part):
        skip = part * QUARTER
        text_hop(f"ax{k}{part}", "x" + way, row_a(0, 0) + skip, row_a(0, k) + skip, QUARTER)
        text_hop(f"by{k}{part}", "y" + way, row_b(0, 0) + skip, row_b(0, k) + skip, QUARTER)

    def image_hop(way, src, dst, part):
        skip = part * QUARTER
        send(f"i{dst}{part}", way, images, row_i(src) + skip, images, row_i(dst) + skip, QUARTER)

    def image_pass(slot):
        send(f"p{slot}", "c", images, row_i(slot), images, row_i(slot, 1), ROWS)

    def image_step(hop, n):
        up, down = n, (n + 2) % 4
        if hop:
            arrived(f"i{hop}{up}", f"i{8 - hop}{down}")
        if hop < 3 or n < 2:
            image_hop("z+", hop, hop + 1, up)
            image_hop("z-", (8 - hop) % 8, 7 - hop, down)

    def spread(k):
        text_hop(f"a1{k}", "y+", row_a(0, k), row_a(1, k))
        text_hop(f"b1{k}", "x+", row_b(0, k), row_b(1, k))
        text_hop(f"a3{k}", "y-", row_a(0, k), row_a(3, k))
        text_hop(f"b3{k}", "x-", row_b(0, k), row_b(3, k))

    def forward(k, way, near_group):
        arrived(f"a{near_group}{k}", f"b{near_group}{k}")
        text_hop(f"a2{k}", "y" + way, row_a(near_group, k), row_a(2, k))
        text_hop(f"b2{k}", "x" + way, row_b(near_group, k), row_b(2, k))

    first_hop(1, "+", 0)
    first_hop(3, "-", 1)
    image_step(0, 0)
    first_hop(1, "+", 1)
    first_hop(3, "-", 0)
    image_step(0, 1)
    image_pass(0)
    spread(0)
    image_step(0, 2)
    image_step(0, 3)

    def score(first, rows, column, width):
        block = texts[pl.ds(column, width), :]
        logits = lax.dot_general(
            images[pl.ds(first, rows), :], block, (((1,), (1,)), ((), ())), preferred_element_type=jnp.float32
        )
        scale_row = jnp.exp(jnp.full((1, width), scale_ref[0], jnp.float32))
        value = 1.0 / (1.0 + jnp.exp(-(scale_row * logits + jnp.full((1, width), bias_ref[0], jnp.float32))))
        if column == 0 and first == 0:
            r = lax.broadcasted_iota(jnp.int32, logits.shape, 0)
            c = lax.broadcasted_iota(jnp.int32, logits.shape, 1)
            same = ((r < HALF) & (c == r)) | ((r >= HALF) & (r < ROWS) & (c == r + (128 - HALF)))
            value = value - same.astype(jnp.float32)
        weight[pl.ds(first, rows), pl.ds(column, width)] = value.astype(jnp.bfloat16)

    arrived("ax10", "by10", "ax31", "by31")
    text_hop("ax20", "x+", row_a(0, 1), row_a(0, 2), QUARTER)
    text_hop("by20", "y+", row_b(0, 1), row_b(0, 2), QUARTER)
    text_hop("ax21", "x-", row_a(0, 3) + QUARTER, row_a(0, 2) + QUARTER, QUARTER)
    text_hop("by21", "y-", row_b(0, 3) + QUARTER, row_b(0, 2) + QUARTER, QUARTER)
    image_step(1, 0)
    arrived("ax11", "by11", "ax30", "by30")
    spread(1)
    spread(3)
    image_step(1, 1)
    image_step(1, 2)
    image_step(1, 3)
    image_pass(1)
    image_pass(7)
    arrived("ax20", "by20", "ax21", "by21")
    spread(2)
    forward(0, "+", 1)
    image_step(2, 0)
    image_step(2, 1)
    arrived("p0", "p1", "p7")
    score(0, 384, 0, GROUP)
    image_step(2, 2)
    forward(1, "+", 1)
    image_step(2, 3)
    image_pass(2)
    image_pass(6)
    arrived("a30", "b30", "a31", "b31")
    score(0, 384, GROUP, GROUP)
    image_step(3, 0)
    forward(3, "-", 3)
    image_step(3, 1)
    forward(2, "-", 3)
    image_step(3, 2)
    image_step(3, 3)
    image_pass(3)
    image_pass(5)
    arrived("p2", "p6")
    score(384, 256, 0, 2 * GROUP)
    arrived("a12", "b12", "a13", "b13")
    score(0, 640, 2 * GROUP, GROUP)
    arrived("i40", "i41", "i42", "i43")
    image_pass(4)
    arrived("p3", "p5")
    score(640, 256, 0, 3 * GROUP)
    arrived("a20", "b20", "a21", "b21", "a23", "b23", "a22", "b22")
    score(0, 896, 3 * GROUP, GROUP)

    landed = {}

    def scatter(name, way, src, src_row, rows):
        landed[name] = used[0]
        send(name, way, src, src_row, landing, used[0], rows)
        used[0] += rows

    def landing_of(name, rows, skip=0):
        return landing[pl.ds(landed[name] + skip, rows), :].astype(jnp.float32)

    def text_back(group, first=0, rows=1024):
        return lax.dot_general(
            weight[pl.ds(first, rows), pl.ds(group * GROUP, GROUP)], images[pl.ds(first, rows), :],
            (((0,), (0,)), ((), ())), preferred_element_type=jnp.float32,
        )

    def image_back(*slots):
        back = jnp.dot(
            weight[pl.ds(row_i(slots[0]), 128 * len(slots)), :], texts[...], preferred_element_type=jnp.float32
        )
        for n, slot in enumerate(slots):
            place = PLACE[slot] * ROWS
            pass_send[pl.ds(place, ROWS), :] = back[n * 128 + ROWS:(n + 1) * 128].astype(jnp.bfloat16)
            scatter(f"q{slot}", "c", pass_send, place, ROWS)
            image_sum[pl.ds(place, ROWS), :] = back[n * 128:n * 128 + ROWS]

    def image_on(slot, way, before, parts):
        for part in parts:
            row = PLACE[slot] * ROWS + part * QUARTER
            total = image_sum[pl.ds(row, QUARTER), :] + landing_of(f"q{slot}", QUARTER, part * QUARTER)
            if before is not None:
                arrived(f"j{before}{part}")
                total = total + landing_of(f"j{before}{part}", QUARTER)
            image_send[pl.ds(row, QUARTER), :] = total.astype(jnp.bfloat16)
            scatter(f"j{slot}{part}", way, image_send, row, QUARTER)

    def text_row(kind, group, k):
        return (row_a if kind == "a" else row_b)(group, k)

    def text_on(group, k, way, before=None):
        for kind, axis in (("a", "y"), ("b", "x")):
            row = text_row(kind, group, k)
            total = text_sum[pl.ds(row, HALF), :]
            if before is not None:
                arrived(f"t{kind}{before}{k}")
                total = total + landing_of(f"t{kind}{before}{k}", HALF)
            text_send[pl.ds(row, HALF), :] = total.astype(jnp.bfloat16)
            scatter(f"t{kind}{group}{k}", axis + way, text_send, row, HALF)

    def reduced(kind, k):
        arrived(f"t{kind}1{k}", f"t{kind}3{k}")
        total = text_sum[pl.ds(text_row(kind, 0, k), HALF), :]
        return (total + landing_of(f"t{kind}1{k}", HALF)) + landing_of(f"t{kind}3{k}", HALF)

    def second_far():
        for kind, axis in (("a", "x"), ("b", "y")):
            row = text_row(kind, 0, 2)
            text_send[pl.ds(row, HALF), :] = reduced(kind, 2).astype(jnp.bfloat16)
            scatter(f"u{kind}2m", axis + "-", text_send, row, QUARTER)
            scatter(f"u{kind}2p", axis + "+", text_send, row + QUARTER, QUARTER)

    def second_near(k, part, way):
        for kind, axis in (("a", "x"), ("b", "y")):
            row = text_row(kind, 0, k)
            total = reduced(kind, k)
            arrived(f"u{kind}2{part}")
            extra = landing_of(f"u{kind}2{part}", QUARTER)
            if part == "m":
                total = jnp.concatenate([total[:QUARTER] + extra, total[QUARTER:]], axis=0)
            else:
                total = jnp.concatenate([total[:QUARTER], total[QUARTER:] + extra], axis=0)
            text_send[pl.ds(row, HALF), :] = total.astype(jnp.bfloat16)
            scatter(f"u{kind}{k}", axis + way, text_send, row, HALF)

    def far_on(k, way):
        scatter(f"ta2{k}", "y" + way, text_send, row_a(2, k), HALF)
        scatter(f"tb2{k}", "x" + way, text_send, row_b(2, k), HALF)

    arrived("p4")
    score(896, 128, 0, 4 * GROUP)
    text_send[pl.ds(3 * GROUP, GROUP), :] = text_back(3).astype(jnp.bfloat16)
    far_on(2, "+")
    far_on(1, "-")
    far_on(3, "+")
    image_back(4)
    image_back(3, 5)
    text_sum[pl.ds(2 * GROUP, GROUP), :] = text_back(2)
    text_on(1, 2, "-")
    far_on(0, "-")
    arrived("q4")
    image_on(4, "z-", None, (0, 1))
    image_on(4, "z+", None, (2, 3))
    text_sum[pl.ds(1 * GROUP, GROUP), :] = text_back(1)
    arrived("q3", "q5")
    image_on(3, "z-", None, (2, 3))
    image_on(5, "z+", None, (0, 1))
    text_on(3, 2, "+", 2)
    text_on(3, 1, "+")
    text_on(1, 1, "-", 2)
    text_on(1, 3, "-")
    image_back(2, 6)
    image_on(3, "z-", 4, (0, 1))
    image_on(5, "z+", 4, (2, 3))
    text_on(3, 3, "+", 2)
    text_sum[pl.ds(0, GROUP), :] = text_back(0)
    arrived("q2", "q6")
    image_on(2, "z-", 3, (2, 3))
    image_on(6, "z+", 5, (0, 1))
    image_back(1, 7)
    second_far()
    image_on(2, "z-", 3, (0, 1))
    image_on(6, "z+", 5, (2, 3))
    text_on(1, 0, "-", 2)
    text_on(3, 0, "+")
    image_back(0)
    arrived("q1", "q7")
    image_on(1, "z-", 2, (2, 3))
    image_on(7, "z+", 6, (0, 1))
    second_near(1, "m", "-")
    second_near(3, "p", "+")
    image_on(1, "z-", 2, (0, 1))
    image_on(7, "z+", 6, (2, 3))

    scale = jnp.exp(jnp.full((1, WIDTH), scale_ref[0], jnp.float32))
    image_unit, image_inv = normalize(image_ref[...])
    arrived("q0")
    for part in range(4):
        arrived(f"j7{part}", f"j1{part}")
    up = jnp.concatenate([landing_of("j70", HALF), landing_of("j72", HALF)], axis=0)
    down = jnp.concatenate([landing_of("j10", HALF), landing_of("j12", HALF)], axis=0)
    back = (image_sum[pl.ds(0, ROWS), :] + landing_of("q0", ROWS)) + (up + down)
    out[pl.ds(0, ROWS), :] = tangent(scale * back, image_unit, image_inv)

    text_unit, text_inv = normalize(text_ref[...])
    for n, kind in enumerate(("a", "b")):
        back = reduced(kind, 0)
        arrived(f"u{kind}1", f"u{kind}3")
        back = (back + landing_of(f"u{kind}1", HALF)) + landing_of(f"u{kind}3", HALF)
        part = slice(n * HALF, (n + 1) * HALF)
        out[pl.ds(ROWS + n * HALF, HALF), :] = tangent(scale * back, text_unit[part], text_inv[part])

    for copy in copies.values():
        copy.wait_send()


COPIES = 144


def per_device(image_raw, text_raw, log_scale, bias):
    block = jax.ShapeDtypeStruct((2 * ROWS, WIDTH), jnp.bfloat16)
    vmem = pl.BlockSpec(memory_space=pltpu.VMEM)
    smem = pl.BlockSpec(memory_space=pltpu.SMEM)
    half, full = jnp.bfloat16, jnp.float32
    both = pl.pallas_call(
        kernel,
        out_shape=block,
        in_specs=[vmem, smem, smem],
        out_specs=vmem,
        scratch_shapes=[
            pltpu.VMEM((1024, WIDTH), half),
            pltpu.VMEM((1024, WIDTH), half),
            pltpu.VMEM((1024, 1024), half),
            pltpu.VMEM((1024, WIDTH), full),
            pltpu.VMEM((512, WIDTH), full),
            pltpu.VMEM((1024, WIDTH), half),
            pltpu.VMEM((512, WIDTH), half),
            pltpu.VMEM((512, WIDTH), half),
            pltpu.VMEM((2048, WIDTH), half),
            pltpu.SemaphoreType.DMA((COPIES,)),
            pltpu.SemaphoreType.DMA((COPIES,)),
        ],
        compiler_params=pltpu.CompilerParams(
            collective_id=0, has_side_effects=True, vmem_limit_bytes=52 * 2**20
        ),
        cost_estimate=pl.CostEstimate(flops=7_300_000_000, bytes_accessed=600_000, transcendentals=1_100_000),
    )(jnp.concatenate([image_raw, text_raw], axis=0), log_scale, bias)
    return both[:ROWS], both[ROWS:]


def solution(mesh):
    rows = P(("grp", "blk"), None)
    return jax.shard_map(
        per_device, mesh=mesh, in_specs=(rows, rows, P(), P()), out_specs=(rows, rows), check_vma=False
    )
```

```python
import functools

import jax
import jax.numpy as jnp
from jax import lax
from jax.experimental import pallas as pl
from jax.experimental.pallas import tpu as pltpu
from jax.sharding import PartitionSpec as P

NX, NY, NZ = 4, 4, 8
ROWS = 64
HALF = 32
QUARTER = 16
WIDTH = 1152
GROUP = 256
PLACE = {0: 0, 1: 1, 7: 2, 2: 3, 6: 4, 3: 5, 5: 6, 4: 7}


def coords():
    grp, blk = lax.axis_index("grp"), lax.axis_index("blk")
    core = lax.rem(grp, 2)
    y = lax.rem(grp // 2, NY)
    x = (blk // NZ) * 2 + grp // 8
    return x, y, lax.rem(blk, NZ), core


def device(x, y, z, core):
    x, y, z = lax.rem(x + NX, NX), lax.rem(y + NY, NY), lax.rem(z + NZ, NZ)
    return (lax.rem(x, 2) * 8 + y * 2 + core, (x // 2) * NZ + z)


def normalize(raw):
    values = raw.astype(jnp.float32)
    inverse = lax.rsqrt(jnp.sum(values * values, axis=-1, keepdims=True) + 1e-06)
    return values * inverse, inverse


def tangent(back, unit, inverse):
    along = jnp.sum(unit * back, axis=-1, keepdims=True)
    return ((back - unit * along) * inverse).astype(jnp.bfloat16)


def text_place(group, k):
    if group in (0, 2):
        return group // 2 * 3 * GROUP + k * HALF
    return (GROUP if k < 2 else 2 * GROUP) + group // 2 * ROWS + k % 2 * HALF


def row_a(dy, dx):
    return text_place(dy, dx)


def row_b(dx, dy):
    return text_place(dx, dy) + 128


def row_i(slot, other=0):
    return PLACE[slot] * 128 + other * ROWS


def kernel(raw_ref, scale_ref, bias_ref, out,
           images, texts, weight, text_sum, image_sum, text_send, pass_send, image_send, landing,
           send_sem, recv_sem):
    image_ref, text_ref = raw_ref.at[pl.ds(0, ROWS)], raw_ref.at[pl.ds(ROWS, ROWS)]
    x, y, z, core = coords()
    near = {
        "x+": device(x + 1, y, z, core), "x-": device(x - 1, y, z, core),
        "y+": device(x, y + 1, z, core), "y-": device(x, y - 1, z, core),
        "z+": device(x, y, z + 1, core), "z-": device(x, y, z - 1, core),
        "c": device(x, y, z, 1 - core),
    }
    barrier = pltpu.get_barrier_semaphore()
    for target in near.values():
        pl.semaphore_signal(barrier, inc=1, device_id=target, device_id_type=pl.DeviceIdType.MESH)

    text_unit, _ = normalize(text_ref[...])
    text_half = text_unit.astype(jnp.bfloat16)
    texts[pl.ds(row_a(0, 0), HALF), :] = text_half[:HALF]
    texts[pl.ds(row_b(0, 0), HALF), :] = text_half[HALF:]
    image_unit, _ = normalize(image_ref[...])
    images[pl.ds(0, ROWS), :] = image_unit.astype(jnp.bfloat16)

    pl.semaphore_wait(barrier, len(near))

    copies = {}
    used = [0]

    def send(name, way, src, src_row, dst, dst_row, rows):
        number = len(copies)
        copy = pltpu.make_async_remote_copy(
            src_ref=src.at[pl.ds(src_row, rows)], dst_ref=dst.at[pl.ds(dst_row, rows)],
            send_sem=send_sem.at[number], recv_sem=recv_sem.at[number],
            device_id=near[way], device_id_type=pl.DeviceIdType.MESH,
        )
        copy.start()
        copies[name] = copy

    def arrived(*names):
        for name in names:
            copies[name].wait_recv()

    def text_hop(name, way, src, dst, rows=HALF):
        send(name, way, texts, src, texts, dst, rows)

    def first_hop(k, way, part):
        skip = part * QUARTER
        text_hop(f"ax{k}{part}", "x" + way, row_a(0, 0) + skip, row_a(0, k) + skip, QUARTER)
        text_hop(f"by{k}{part}", "y" + way, row_b(0, 0) + skip, row_b(0, k) + skip, QUARTER)

    def image_hop(way, src, dst, part):
        skip = part * QUARTER
        send(f"i{dst}{part}", way, images, row_i(src) + skip, images, row_i(dst) + skip, QUARTER)

    def image_pass(slot):
        send(f"p{slot}", "c", images, row_i(slot), images, row_i(slot, 1), ROWS)

    def image_step(hop, n):
        up, down = n, (n + 2) % 4
        if hop:
            arrived(f"i{hop}{up}", f"i{8 - hop}{down}")
        if hop < 3 or n < 2:
            image_hop("z+", hop, hop + 1, up)
            image_hop("z-", (8 - hop) % 8, 7 - hop, down)

    def spread(k):
        text_hop(f"a1{k}", "y+", row_a(0, k), row_a(1, k))
        text_hop(f"b1{k}", "x+", row_b(0, k), row_b(1, k))
        text_hop(f"a3{k}", "y-", row_a(0, k), row_a(3, k))
        text_hop(f"b3{k}", "x-", row_b(0, k), row_b(3, k))

    def forward(k, way, near_group):
        arrived(f"a{near_group}{k}", f"b{near_group}{k}")
        text_hop(f"a2{k}", "y" + way, row_a(near_group, k), row_a(2, k))
        text_hop(f"b2{k}", "x" + way, row_b(near_group, k), row_b(2, k))

    first_hop(1, "+", 0)
    first_hop(3, "-", 1)
    image_step(0, 0)
    first_hop(1, "+", 1)
    first_hop(3, "-", 0)
    image_step(0, 1)
    image_pass(0)
    spread(0)
    image_step(0, 2)
    image_step(0, 3)

    def score(first, rows, column, width):
        block = texts[pl.ds(column, width), :]
        logits = lax.dot_general(
            images[pl.ds(first, rows), :], block, (((1,), (1,)), ((), ())), preferred_element_type=jnp.float32
        )
        scale_row = jnp.exp(jnp.full((1, width), scale_ref[0], jnp.float32))
        value = 1.0 / (1.0 + jnp.exp(-(scale_row * logits + jnp.full((1, width), bias_ref[0], jnp.float32))))
        if column == 0 and first == 0:
            r = lax.broadcasted_iota(jnp.int32, logits.shape, 0)
            c = lax.broadcasted_iota(jnp.int32, logits.shape, 1)
            same = ((r < HALF) & (c == r)) | ((r >= HALF) & (r < ROWS) & (c == r + (128 - HALF)))
            value = value - same.astype(jnp.float32)
        weight[pl.ds(first, rows), pl.ds(column, width)] = value.astype(jnp.bfloat16)

    arrived("ax10", "by10", "ax31", "by31")
    text_hop("ax20", "x+", row_a(0, 1), row_a(0, 2), QUARTER)
    text_hop("by20", "y+", row_b(0, 1), row_b(0, 2), QUARTER)
    text_hop("ax21", "x-", row_a(0, 3) + QUARTER, row_a(0, 2) + QUARTER, QUARTER)
    text_hop("by21", "y-", row_b(0, 3) + QUARTER, row_b(0, 2) + QUARTER, QUARTER)
    image_step(1, 0)
    arrived("ax11", "by11", "ax30", "by30")
    spread(1)
    spread(3)
    image_step(1, 1)
    image_step(1, 2)
    image_step(1, 3)
    image_pass(1)
    image_pass(7)
    arrived("ax20", "by20", "ax21", "by21")
    spread(2)
    forward(0, "+", 1)
    image_step(2, 0)
    image_step(2, 1)
    image_step(2, 2)
    forward(1, "+", 1)
    image_step(2, 3)
    image_pass(2)
    image_pass(6)
    arrived("p0", "p1", "p7", "a30", "b30", "a31", "b31")
    score(0, 384, 0, 2 * GROUP)
    image_step(3, 0)
    forward(3, "-", 3)
    image_step(3, 1)
    forward(2, "-", 3)
    image_step(3, 2)
    image_step(3, 3)
    image_pass(3)
    image_pass(5)
    arrived("p2", "p6")
    score(384, 256, 0, 2 * GROUP)
    arrived("a12", "b12", "a13", "b13")
    score(0, 640, 2 * GROUP, GROUP)
    arrived("i40", "i41", "i42", "i43")
    image_pass(4)
    arrived("p3", "p5")
    score(640, 256, 0, 3 * GROUP)
    arrived("a20", "b20", "a21", "b21", "a23", "b23", "a22", "b22")
    score(0, 896, 3 * GROUP, GROUP)

    landed = {}

    def scatter(name, way, src, src_row, rows):
        landed[name] = used[0]
        send(name, way, src, src_row, landing, used[0], rows)
        used[0] += rows

    def landing_of(name, rows, skip=0):
        return landing[pl.ds(landed[name] + skip, rows), :].astype(jnp.float32)

    def text_back(group, first=0, rows=1024):
        return lax.dot_general(
            weight[pl.ds(first, rows), pl.ds(group * GROUP, GROUP)], images[pl.ds(first, rows), :],
            (((0,), (0,)), ((), ())), preferred_element_type=jnp.float32,
        )

    def image_back(*slots):
        back = jnp.dot(
            weight[pl.ds(row_i(slots[0]), 128 * len(slots)), :], texts[...], preferred_element_type=jnp.float32
        )
        for n, slot in enumerate(slots):
            place = PLACE[slot] * ROWS
            pass_send[pl.ds(place, ROWS), :] = back[n * 128 + ROWS:(n + 1) * 128].astype(jnp.bfloat16)
            scatter(f"q{slot}", "c", pass_send, place, ROWS)
            image_sum[pl.ds(place, ROWS), :] = back[n * 128:n * 128 + ROWS]

    def image_on(slot, way, before, parts):
        for part in parts:
            row = PLACE[slot] * ROWS + part * QUARTER
            total = image_sum[pl.ds(row, QUARTER), :] + landing_of(f"q{slot}", QUARTER, part * QUARTER)
            if before is not None:
                arrived(f"j{before}{part}")
                total = total + landing_of(f"j{before}{part}", QUARTER)
            image_send[pl.ds(row, QUARTER), :] = total.astype(jnp.bfloat16)
            scatter(f"j{slot}{part}", way, image_send, row, QUARTER)

    def text_row(kind, group, k):
        return (row_a if kind == "a" else row_b)(group, k)

    def text_on(group, k, way, before=None):
        for kind, axis in (("a", "y"), ("b", "x")):
            row = text_row(kind, group, k)
            total = text_sum[pl.ds(row, HALF), :]
            if before is not None:
                arrived(f"t{kind}{before}{k}")
                total = total + landing_of(f"t{kind}{before}{k}", HALF)
            text_send[pl.ds(row, HALF), :] = total.astype(jnp.bfloat16)
            scatter(f"t{kind}{group}{k}", axis + way, text_send, row, HALF)

    def reduced(kind, k):
        arrived(f"t{kind}1{k}", f"t{kind}3{k}")
        total = text_sum[pl.ds(text_row(kind, 0, k), HALF), :]
        return (total + landing_of(f"t{kind}1{k}", HALF)) + landing_of(f"t{kind}3{k}", HALF)

    def second_far():
        for kind, axis in (("a", "x"), ("b", "y")):
            row = text_row(kind, 0, 2)
            text_send[pl.ds(row, HALF), :] = reduced(kind, 2).astype(jnp.bfloat16)
            scatter(f"u{kind}2m", axis + "-", text_send, row, QUARTER)
            scatter(f"u{kind}2p", axis + "+", text_send, row + QUARTER, QUARTER)

    def second_near(k, part, way):
        for kind, axis in (("a", "x"), ("b", "y")):
            row = text_row(kind, 0, k)
            total = reduced(kind, k)
            arrived(f"u{kind}2{part}")
            extra = landing_of(f"u{kind}2{part}", QUARTER)
            if part == "m":
                total = jnp.concatenate([total[:QUARTER] + extra, total[QUARTER:]], axis=0)
            else:
                total = jnp.concatenate([total[:QUARTER], total[QUARTER:] + extra], axis=0)
            text_send[pl.ds(row, HALF), :] = total.astype(jnp.bfloat16)
            scatter(f"u{kind}{k}", axis + way, text_send, row, HALF)

    def far_on(k, way):
        scatter(f"ta2{k}", "y" + way, text_send, row_a(2, k), HALF)
        scatter(f"tb2{k}", "x" + way, text_send, row_b(2, k), HALF)

    arrived("p4")
    score(896, 128, 0, 4 * GROUP)
    text_send[pl.ds(3 * GROUP, GROUP), :] = text_back(3).astype(jnp.bfloat16)
    far_on(2, "+")
    far_on(1, "-")
    far_on(3, "+")
    image_back(4)
    image_back(3, 5)
    text_sum[pl.ds(2 * GROUP, GROUP), :] = text_back(2)
    text_on(1, 2, "-")
    far_on(0, "-")
    arrived("q4")
    image_on(4, "z-", None, (0, 1))
    image_on(4, "z+", None, (2, 3))
    text_sum[pl.ds(1 * GROUP, GROUP), :] = text_back(1)
    arrived("q3", "q5")
    image_on(3, "z-", None, (2, 3))
    image_on(5, "z+", None, (0, 1))
    text_on(3, 2, "+", 2)
    text_on(3, 1, "+")
    text_on(1, 1, "-", 2)
    text_on(1, 3, "-")
    image_back(2, 6)
    image_on(3, "z-", 4, (0, 1))
    image_on(5, "z+", 4, (2, 3))
    text_on(3, 3, "+", 2)
    text_sum[pl.ds(0, GROUP), :] = text_back(0)
    arrived("q2", "q6")
    image_on(2, "z-", 3, (2, 3))
    image_on(6, "z+", 5, (0, 1))
    image_back(1, 7)
    second_far()
    image_on(2, "z-", 3, (0, 1))
    image_on(6, "z+", 5, (2, 3))
    text_on(1, 0, "-", 2)
    text_on(3, 0, "+")
    image_back(0)
    arrived("q1", "q7")
    image_on(1, "z-", 2, (2, 3))
    image_on(7, "z+", 6, (0, 1))
    second_near(1, "m", "-")
    second_near(3, "p", "+")
    image_on(1, "z-", 2, (0, 1))
    image_on(7, "z+", 6, (2, 3))

    scale = jnp.exp(jnp.full((1, WIDTH), scale_ref[0], jnp.float32))
    image_unit, image_inv = normalize(image_ref[...])
    arrived("q0")
    for part in range(4):
        arrived(f"j7{part}", f"j1{part}")
    up = jnp.concatenate([landing_of("j70", HALF), landing_of("j72", HALF)], axis=0)
    down = jnp.concatenate([landing_of("j10", HALF), landing_of("j12", HALF)], axis=0)
    back = (image_sum[pl.ds(0, ROWS), :] + landing_of("q0", ROWS)) + (up + down)
    out[pl.ds(0, ROWS), :] = tangent(scale * back, image_unit, image_inv)

    text_unit, text_inv = normalize(text_ref[...])
    for n, kind in enumerate(("a", "b")):
        back = reduced(kind, 0)
        arrived(f"u{kind}1", f"u{kind}3")
        back = (back + landing_of(f"u{kind}1", HALF)) + landing_of(f"u{kind}3", HALF)
        part = slice(n * HALF, (n + 1) * HALF)
        out[pl.ds(ROWS + n * HALF, HALF), :] = tangent(scale * back, text_unit[part], text_inv[part])

    for copy in copies.values():
        copy.wait_send()


COPIES = 144


def per_device(image_raw, text_raw, log_scale, bias):
    block = jax.ShapeDtypeStruct((2 * ROWS, WIDTH), jnp.bfloat16)
    vmem = pl.BlockSpec(memory_space=pltpu.VMEM)
    smem = pl.BlockSpec(memory_space=pltpu.SMEM)
    half, full = jnp.bfloat16, jnp.float32
    both = pl.pallas_call(
        kernel,
        out_shape=block,
        in_specs=[vmem, smem, smem],
        out_specs=vmem,
        scratch_shapes=[
            pltpu.VMEM((1024, WIDTH), half),
            pltpu.VMEM((1024, WIDTH), half),
            pltpu.VMEM((1024, 1024), half),
            pltpu.VMEM((1024, WIDTH), full),
            pltpu.VMEM((512, WIDTH), full),
            pltpu.VMEM((1024, WIDTH), half),
            pltpu.VMEM((512, WIDTH), half),
            pltpu.VMEM((512, WIDTH), half),
            pltpu.VMEM((2048, WIDTH), half),
            pltpu.SemaphoreType.DMA((COPIES,)),
            pltpu.SemaphoreType.DMA((COPIES,)),
        ],
        compiler_params=pltpu.CompilerParams(
            collective_id=0, has_side_effects=True, vmem_limit_bytes=52 * 2**20
        ),
        cost_estimate=pl.CostEstimate(flops=7_300_000_000, bytes_accessed=600_000, transcendentals=1_100_000),
    )(jnp.concatenate([image_raw, text_raw], axis=0), log_scale, bias)
    return both[:ROWS], both[ROWS:]


def solution(mesh):
    rows = P(("grp", "blk"), None)
    return jax.shard_map(
        per_device, mesh=mesh, in_specs=(rows, rows, P(), P()), out_specs=(rows, rows), check_vma=False
    )
```
